512 devices in a mesh: seq: 64 (over z, y_hi, x), grp: 8 (over y_lo, core).
Axes of the slice: x: 4, y: 8 (y_hi: 2, y_lo: 4; y = y_hi * 4 + y_lo), z: 8, core: 2. Of those that a mesh axis runs over, the one named last changes fastest.
Arguments:
- inner_input: bfloat16 [65536, 4096], P(('seq', 'grp')), may hold values from -6 to 6
- inner_gate: bfloat16 [65536, 4096], P(('seq', 'grp')), may hold values from -6 to 6
- conv_weight: float32 [2, 4, 4096], P(None, None, 'grp'), may hold values from -3 to 3
- conv_bias: float32 [2, 4096], P(None, 'grp'), may hold values from -1.5 to 0.5
- proj_weight: bfloat16 [2, 4096, 160], P(None, 'grp'), may hold values from -0.0625 to 0.0625
- step_weight: bfloat16 [2, 128, 4096], P(None, None, 'grp'), may hold values from -0.5 to 0.5
- step_bias: float32 [2, 4096], P(None, 'grp'), may hold values from -12 to 1
- decay_rate: float32 [2, 16, 4096], P(None, None, 'grp'), may hold values from 0.02 to 0.1
- skip_gain: float32 [2, 4096], P(None, 'grp'), may hold values from 0.5 to 1.5
Outputs:
- gated: bfloat16 [65536, 4096], P(('seq', 'grp'))
The draws below stay inside these ranges and needn't reach their ends.
All inputs are finite; a program needn't handle non-finite values.
Results may differ from the reference program's by a relative error of at most 0.012.
Values may be sent and summed in bfloat16 or wider, within the bound.
A program may use at most 128 MiB of HBM per device.

```python
import math
import jax
import jax.numpy as jnp
from jax import lax

E = 4096
R = 128
N = 16
KERNEL = 4
LEN = 65536
P_SIZE = 160


def draw_proj_weight(key, part):
    key = jax.random.fold_in(key, 5)
    values = jnp.clip(jax.random.normal(key, (2, E, P_SIZE), jnp.float32), -4.0, 4.0)
    column = jnp.arange(P_SIZE)
    factor = jnp.where((column >= R) & (column < R + N), 0.2, 1.0)
    return (values * factor[None, None, :] / math.sqrt(E)).astype(jnp.bfloat16)


def draw_step_bias(key, part):
    key = jax.random.fold_in(key, 7)
    flag_key, slow_key, fast_key = jax.random.split(key, 3)
    share = 0.5
    slow = jax.random.bernoulli(flag_key, share, (2, E))
    slow_bias = math.log(12.0 / LEN) + jax.random.uniform(slow_key, (2, E), jnp.float32) * math.log(10.0)
    fast_bias = jax.random.uniform(fast_key, (2, E), jnp.float32, -1.0, 1.0)
    return jnp.where(slow, slow_bias, fast_bias).astype(jnp.float32)


def block_levels(key, shape, cuts, low, top_value):
    level = 1.0
    for dim, blocks in cuts:
        draws = jax.random.uniform(jax.random.fold_in(jax.random.fold_in(key, 6), dim), (blocks,), jnp.float32, low / len(cuts), top_value / len(cuts))
        level = level * jnp.repeat(jnp.exp(draws), shape[dim] // blocks).reshape((-1,) + (1,) * (len(shape) - 1 - dim))
    return level


def gaussian(stream_key, extent, spread, bound, shards=(), held_as=jnp.bfloat16):
    values = spread * jax.random.normal(stream_key, extent, jnp.float32)
    if shards:
        values = values * block_levels(stream_key, extent, shards, -0.22, 0.18)
    return jnp.clip(values, -bound, bound).astype(held_as)


def setup_inputs(seed: int = 0) -> dict:
    streams_of = jax.random.split(jax.random.key(seed), 10)
    inner_input = gaussian(streams_of[0], (LEN, E), 1.0, 6.0, ((0, 512),))
    inner_gate = gaussian(streams_of[1], (LEN, E), 1.0, 6.0, ((0, 512),))
    conv_weight = gaussian(streams_of[2], (2, KERNEL, E), KERNEL ** -0.5, 3.0, ((2, 8),), jnp.float32)
    conv_bias = jnp.clip(-1.5 + 2.0 * jax.random.uniform(streams_of[3], (2, E), jnp.float32) ** block_levels(streams_of[3], (2, E), ((1, 8),), -0.2, 0.2), -1.5, 0.5)
    proj_weight = draw_proj_weight(jax.random.fold_in(streams_of[9], 71), 0)
    step_weight = gaussian(streams_of[5], (2, R, E), R ** -0.5, 0.5, ((2, 8),))
    step_bias = draw_step_bias(jax.random.fold_in(streams_of[9], 71), 0)
    decay_rate = jnp.clip(jnp.exp(math.log(0.1) - 1.609438 * jax.random.uniform(streams_of[7], (2, N, E), jnp.float32) ** block_levels(streams_of[7], (2, N, E), ((2, 8),), -0.2, 0.2)), 0.02, 0.1)
    skip_gain = jnp.clip(1.0 + 0.1 * jax.random.normal(streams_of[8], (2, E), jnp.float32), 0.5, 1.5)
    return {"inner_input": inner_input, "inner_gate": inner_gate, "conv_weight": conv_weight, "conv_bias": conv_bias, "proj_weight": proj_weight, "step_weight": step_weight, "step_bias": step_bias, "decay_rate": decay_rate, "skip_gain": skip_gain}


def conv_silu(values, weight, bias):
    length = values.shape[0]
    kernel = weight.shape[0]
    padded = jnp.concatenate([jnp.zeros((kernel - 1, values.shape[1]), values.dtype), values], 0)
    summed = jnp.zeros(values.shape, jnp.float32) + bias.astype(jnp.float32)[None]
    for position in range(kernel):
        summed = summed + weight[position].astype(jnp.float32)[None] * padded[position:position + length].astype(jnp.float32)
    return jax.nn.silu(summed).astype(jnp.bfloat16)


def branch_output(values, weight, bias, projection, step_proj, step_shift, rates, direct):
    length, width = values.shape
    activation = conv_silu(values, weight, bias)
    projected = jnp.dot(activation, projection, preferred_element_type=jnp.float32).astype(jnp.bfloat16)
    low = projected[:, :R]
    in_map = projected[:, R:R + N].astype(jnp.float32)
    out_map = projected[:, R + N:].astype(jnp.float32)
    block_rows = 256
    count = length // block_rows

    def advance(carried, pieces):
        low_rows, in_rows, out_rows, act_rows = pieces
        step_rows = jax.nn.softplus(jnp.dot(low_rows, step_proj, preferred_element_type=jnp.float32) + step_shift[None])
        act_float = act_rows.astype(jnp.float32)

        def single(state, row):
            step_row, in_row, out_row, act_row = row
            state = jnp.exp(-step_row[None] * rates) * state + (step_row * act_row)[None] * in_row[:, None]
            return state, jnp.sum(out_row[:, None] * state, axis=0)

        carried, outputs = lax.scan(single, carried, (step_rows, in_rows, out_rows, act_float))
        return carried, outputs + direct[None] * act_float

    pieces = (low.reshape(count, block_rows, R), in_map.reshape(count, block_rows, N),
              out_map.reshape(count, block_rows, N), activation.reshape(count, block_rows, width))
    start = jnp.zeros((N, width), jnp.float32)
    unused, outputs = lax.scan(advance, start, pieces)
    return outputs.reshape(length, width)


def reference(inner_input, inner_gate, conv_weight, conv_bias, proj_weight, step_weight, step_bias, decay_rate, skip_gain):
    forward = branch_output(inner_input, conv_weight[0], conv_bias[0], proj_weight[0], step_weight[0], step_bias[0], decay_rate[0], skip_gain[0])
    reverse = branch_output(jnp.flip(inner_input, 0), conv_weight[1], conv_bias[1], proj_weight[1], step_weight[1], step_bias[1], decay_rate[1], skip_gain[1])
    mixed = (forward + jnp.flip(reverse, 0)).astype(jnp.bfloat16)
    return (mixed.astype(jnp.float32) * jax.nn.silu(inner_gate.astype(jnp.float32))).astype(jnp.bfloat16)
```

```python
import functools
import math

import jax
import jax.numpy as jnp
from jax import lax
from jax.experimental import pallas as pl
from jax.experimental.pallas import tpu as pltpu
from jax.sharding import PartitionSpec as P

F32 = jnp.float32
BF16 = jnp.bfloat16
LOG2E = math.log2(math.e)
LN2 = math.log(2.0)

CHUNKS = 8
LANES = 128

ROW_CONV = 0
ROW_BIAS = 8
ROW_STEP = 10
ROW_SKIP = 12
ROW_RATE = 16
ROWS_SMALL = 48


def iota(shape, dim):
    return lax.broadcasted_iota(jnp.int32, shape, dim)


def silu(value):
    half = 0.5 * value
    return half + half * jnp.tanh(half)


def softplus(value):
    small = jnp.exp2(jnp.abs(value) * -LOG2E)
    series = small * (1.0 - small * (0.5 - small * (1.0 / 3.0 - small * 0.25)))
    logarithm = LN2 * jnp.log2(1.0 + small)
    return jnp.maximum(value, 0.0) + jnp.where(small < 0.02, series, logarithm)


def dot_t(a, b):
    return lax.dot_general(a, b, (((1,), (1,)), ((), ())), preferred_element_type=F32)


def convolve(tile, x_ref, before_ref, after_ref, small_ref, u_ref, rows_f32):
    rows = x_ref.shape[0]
    steps = rows // CHUNKS
    shard, column = tile // 4, lax.rem(tile, 4)
    cols = pl.ds(pl.multiple_of(tile * LANES, LANES), LANES)
    lanes = pl.ds(pl.multiple_of(column * LANES, LANES), LANES)
    rows_f32[0:16, :] = before_ref[:, cols].astype(F32)
    rows_f32[16 : 16 + rows, :] = x_ref[:, cols].astype(F32)
    rows_f32[16 + rows : 32 + rows, :] = after_ref[:, cols].astype(F32)
    taps = {t: rows_f32[pl.ds(16 + t, CHUNKS, stride=steps), :] for t in range(-3, steps + 3)}
    for branch in range(2):
        weights = [
            jnp.broadcast_to(
                small_ref[shard, ROW_CONV + 4 * branch + j : ROW_CONV + 4 * branch + j + 1, lanes],
                (CHUNKS, LANES),
            )
            for j in range(4)
        ]
        bias = jnp.broadcast_to(
            small_ref[shard, ROW_BIAS + branch : ROW_BIAS + branch + 1, lanes], (CHUNKS, LANES)
        )
        sign = -1 if branch == 0 else 1
        for t in range(0, steps, 2):
            pair = []
            for s in (t, t + 1):
                total = bias
                for j in range(4):
                    total = total + weights[j] * taps[s + sign * (3 - j)]
                pair.append(silu(total))
            u_ref[branch, t * CHUNKS : (t + 2) * CHUNKS, cols] = jnp.concatenate(pair, 0).astype(
                BF16
            )


def spread_maps(branch, maps, in_wide, out_wide, out_half):
    rows = maps.shape[0]
    count = rows * 16
    r, c = iota((count, rows), 0), iota((count, rows), 1)
    pick = ((r >> 7) * CHUNKS + (r & 7) == c).astype(F32).astype(BF16)
    picked = jnp.dot(pick, maps, preferred_element_type=F32)
    r, c = iota((count, 32), 0), iota((count, 32), 1)
    state = (r >> 3) & 15
    ones = jnp.ones((32, LANES), BF16)
    in_wide[branch] = jnp.dot(
        jnp.where(state == c, picked, 0.0).astype(BF16), ones, preferred_element_type=F32
    )
    out_wide[branch] = jnp.dot(
        jnp.where(state + 16 == c, picked, 0.0).astype(BF16), ones, preferred_element_type=F32
    )
    r, c = iota((count, rows), 0), iota((count, rows), 1)
    pick = ((r >> 8) * 16 + (r & 15) == c).astype(F32).astype(BF16)
    picked = jnp.dot(pick, maps, preferred_element_type=F32)
    r, c = iota((count, 32), 0), iota((count, 32), 1)
    state = (r >> 4) & 15
    out_half[branch] = jnp.dot(
        jnp.where(state + 16 == c, picked, 0.0).astype(BF16), ones, preferred_element_type=F32
    ).astype(BF16)


def step_sizes(branch, shard, low, step_weight_ref, small_ref, step_ref):
    width = step_weight_ref.shape[-1]
    rows = low.shape[0]
    for q in range(width // LANES):
        lanes = slice(q * LANES, (q + 1) * LANES)
        value = jnp.dot(low, step_weight_ref[shard, branch, :, lanes], preferred_element_type=F32)
        value = value + small_ref[shard, ROW_STEP + branch : ROW_STEP + branch + 1, lanes]
        step_ref[branch, shard * (width // LANES) + q] = softplus(value).reshape(
            rows // CHUNKS, CHUNKS, LANES
        )


def scan_tile(branch, tile, u_ref, small_ref, step_ref, in_wide, out_wide, y_ref, end_ref):
    steps = step_ref.shape[2]
    shard, column = tile // 4, lax.rem(tile, 4)
    cols = pl.ds(pl.multiple_of(tile * LANES, LANES), LANES)
    lanes = pl.ds(pl.multiple_of(column * LANES, LANES), LANES)
    first = ROW_RATE + 16 * branch
    skip = jnp.broadcast_to(
        small_ref[shard, ROW_SKIP + branch : ROW_SKIP + branch + 1, lanes], (CHUNKS, LANES)
    )
    for start in (0, 8):
        rates = jnp.stack(
            [
                jnp.broadcast_to(
                    small_ref[shard, first + n : first + n + 1, lanes], (CHUNKS, LANES)
                )
                for n in range(start, start + 8)
            ]
        )
        state = jnp.zeros((8, CHUNKS, LANES), F32)
        for j in range(steps):
            t = j if branch == 0 else steps - 1 - j
            size = step_ref[branch, tile, t]
            u = u_ref[branch, pl.ds(t * CHUNKS, CHUNKS), cols].astype(F32)
            at = pl.ds((t * 16 + start) * CHUNKS, 8 * CHUNKS)
            into = in_wide[branch, at, :].reshape(8, CHUNKS, LANES)
            out = out_wide[branch, at, :].reshape(8, CHUNKS, LANES)
            state = jnp.exp2(rates * size[None]) * state + (size * u)[None] * into
            part = jnp.sum(out * state, axis=0)
            if start == 0:
                part = part + skip * u
            if branch == 1 or start > 0:
                part = part + y_ref[tile, t]
            y_ref[tile, t] = part
        end_ref[branch, tile, start * CHUNKS : (start + 8) * CHUNKS, :] = state.reshape(
            8 * CHUNKS, LANES
        )


def chunk_totals(branch, tile, step_ref):
    total = step_ref[branch, tile, 0]
    for t in range(1, step_ref.shape[2]):
        total = total + step_ref[branch, tile, t]
    return total


def device_state(branch, tile, small_ref, step_ref, end_ref, totals, state_ref, elapsed_ref):
    shard, column = tile // 4, lax.rem(tile, 4)
    lanes = pl.ds(pl.multiple_of(column * LANES, LANES), LANES)
    first = ROW_RATE + 16 * branch
    rates = small_ref[shard, first : first + 16, lanes]
    totals[...] = chunk_totals(branch, tile, step_ref)
    state = jnp.zeros((16, LANES), F32)
    elapsed = jnp.zeros((1, LANES), F32)
    for j in range(CHUNKS):
        k = j if branch == 0 else CHUNKS - 1 - j
        span = totals[k : k + 1, :]
        state = jnp.exp2(rates * span) * state + end_ref[branch, tile, pl.ds(k, 16, stride=CHUNKS), :]
        elapsed = elapsed + span
    state_ref[branch, tile] = state
    elapsed_ref[branch, tile] = jnp.broadcast_to(elapsed, (8, LANES))


def front_kernel(
    x_ref, before_ref, after_ref, small_ref, proj_weight_ref, step_weight_ref,
    y_ref, end_ref, step_ref, state_ref, elapsed_ref, out_half,
    u_ref, rows_f32, in_wide, out_wide, totals,
):
    tiles = x_ref.shape[1] // LANES
    shards = small_ref.shape[0]

    def conv_body(tile, _):
        convolve(tile, x_ref, before_ref, after_ref, small_ref, u_ref, rows_f32)
        return 0

    lax.fori_loop(0, tiles, conv_body, 0)
    width = proj_weight_ref.shape[-1]
    for branch in range(2):
        projected = jnp.zeros((x_ref.shape[0], proj_weight_ref.shape[2]), F32)
        for shard in range(shards):
            projected = projected + dot_t(
                u_ref[branch, :, shard * width : (shard + 1) * width], proj_weight_ref[shard, branch]
            )
        projected = projected.astype(BF16)
        spread_maps(branch, projected[:, 128:160], in_wide, out_wide, out_half)
        low = projected[:, 0:128]

        def step_body(shard, _):
            step_sizes(branch, shard, low, step_weight_ref, small_ref, step_ref)
            return 0

        lax.fori_loop(0, shards, step_body, 0)

        def scan_body(tile, _):
            scan_tile(
                branch, tile, u_ref, small_ref, step_ref, in_wide, out_wide, y_ref, end_ref
            )
            return 0

        lax.fori_loop(0, tiles, scan_body, 0)

        def state_body(tile, _):
            device_state(
                branch, tile, small_ref, step_ref, end_ref, totals, state_ref, elapsed_ref
            )
            return 0

        lax.fori_loop(0, tiles, state_body, 0)


def correct_tile(
    branch, tile, small_ref, step_ref, end_ref, out_half, carry_ref, y_ref, totals, chunk_carry
):
    shard, column = tile // 4, lax.rem(tile, 4)
    lanes = pl.ds(pl.multiple_of(column * LANES, LANES), LANES)
    first = ROW_RATE + 16 * branch
    steps = step_ref.shape[2]
    rates = small_ref[shard, first : first + 16, lanes]
    totals[...] = chunk_totals(branch, tile, step_ref)
    carry = carry_ref[branch, tile]
    for j in range(CHUNKS):
        k = j if branch == 0 else CHUNKS - 1 - j
        chunk_carry[pl.ds(k, 16, stride=CHUNKS), :] = carry
        if j < CHUNKS - 1:
            carry = (
                jnp.exp2(rates * totals[k : k + 1, :]) * carry
                + end_ref[branch, tile, pl.ds(k, 16, stride=CHUNKS), :]
            )
    entering = []
    wide = []
    for n in range(16):
        one = chunk_carry[n * CHUNKS : (n + 1) * CHUNKS, :]
        entering.append(jnp.concatenate([one, one], 0).astype(BF16))
        rate = small_ref[shard, first + n : first + n + 1, lanes]
        wide.append(jnp.broadcast_to(rate, (16, LANES)).astype(BF16))
    elapsed = jnp.zeros((CHUNKS, LANES), F32)
    for j in range(0, steps, 2):
        pair = []
        for i in (j, j + 1):
            t = i if branch == 0 else steps - 1 - i
            elapsed = elapsed + step_ref[branch, tile, t]
            pair.append(elapsed)
        low = j if branch == 0 else steps - 2 - j
        if branch == 1:
            pair = pair[::-1]
        spans = jnp.concatenate(pair, 0).astype(BF16)
        total = None
        for n in range(16):
            at = (low // 2 * 16 + n) * 16
            part = jnp.exp2(wide[n] * spans) * entering[n] * out_half[branch, at : at + 16, :]
            total = part if total is None else total + part
        total = total.astype(F32)
        y_ref[tile, low] = y_ref[tile, low] + total[:CHUNKS]
        y_ref[tile, low + 1] = y_ref[tile, low + 1] + total[CHUNKS:]


def gate_tile(tile, y_ref, gate_ref, result_ref, rows_f32):
    steps = y_ref.shape[1]
    rows = gate_ref.shape[0]
    cols = pl.ds(pl.multiple_of(tile * LANES, LANES), LANES)
    for t in range(steps):
        rows_f32[pl.ds(t, CHUNKS, stride=steps), :] = y_ref[tile, t]
    mixed = rows_f32[0:rows, :].astype(BF16).astype(F32)
    result_ref[:, cols] = (mixed * silu(gate_ref[:, cols].astype(F32))).astype(BF16)


def back_kernel(
    y_in_ref, end_ref, step_ref, out_half, small_ref, carry_ref, gate_ref, result_ref,
    y_ref, rows_f32, totals, chunk_carry,
):
    tiles = y_in_ref.shape[0]

    def body(tile, _):
        y_ref[tile] = y_in_ref[tile]
        for branch in range(2):
            correct_tile(
                branch, tile, small_ref, step_ref, end_ref, out_half, carry_ref, y_ref, totals,
                chunk_carry,
            )
        gate_tile(tile, y_ref, gate_ref, result_ref, rows_f32)
        return 0

    lax.fori_loop(0, tiles, body, 0)


VMEM = pl.BlockSpec(memory_space=pltpu.VMEM)


def run_front(x, before, after, small, proj_weight, step_weight):
    rows, channels = x.shape
    tiles, steps = channels // LANES, rows // CHUNKS
    shape = jax.ShapeDtypeStruct
    return pl.pallas_call(
        front_kernel,
        out_shape=(
            shape((tiles, steps, CHUNKS, LANES), F32),
            shape((2, tiles, 16 * CHUNKS, LANES), F32),
            shape((2, tiles, steps, CHUNKS, LANES), F32),
            shape((2, tiles, 16, LANES), F32),
            shape((2, tiles, 8, LANES), F32),
            shape((2, rows * 16, LANES), BF16),
        ),
        in_specs=[VMEM] * 6,
        out_specs=(VMEM,) * 6,
        scratch_shapes=[
            pltpu.VMEM((2, rows, channels), BF16),
            pltpu.VMEM((rows + 32, LANES), F32),
            pltpu.VMEM((2, rows * 16, LANES), F32),
            pltpu.VMEM((2, rows * 16, LANES), F32),
            pltpu.VMEM((CHUNKS, LANES), F32),
        ],
        compiler_params=pltpu.CompilerParams(vmem_limit_bytes=56 << 20),
    )(x, before, after, small, proj_weight, step_weight)


def run_back(y, end, step, out_half, small, carry, gate):
    rows, channels = gate.shape
    return pl.pallas_call(
        back_kernel,
        out_shape=jax.ShapeDtypeStruct((rows, channels), BF16),
        in_specs=[VMEM] * 7,
        out_specs=VMEM,
        scratch_shapes=[
            pltpu.VMEM(y.shape, F32),
            pltpu.VMEM((rows + 32, LANES), F32),
            pltpu.VMEM((CHUNKS, LANES), F32),
            pltpu.VMEM((16 * CHUNKS, LANES), F32),
        ],
        compiler_params=pltpu.CompilerParams(vmem_limit_bytes=56 << 20),
    )(y, end, step, out_half, small, carry, gate)


def entering_states(state, elapsed, decay_rate):
    tiles = state.shape[1]
    grp = lax.axis_size("grp")
    seq = lax.axis_size("seq")
    width = tiles // grp
    here_g, here_s = lax.axis_index("grp"), lax.axis_index("seq")
    states = state.reshape(2, grp, width, 16, LANES).transpose(1, 0, 2, 3, 4)
    spans = elapsed.reshape(2, grp, width, 1, LANES).transpose(1, 0, 2, 3, 4)
    both = jnp.concatenate([states, spans], 3)
    both = lax.all_to_all(both, "grp", split_axis=0, concat_axis=0, tiled=True)
    rates = decay_rate.reshape(2, 16, width, LANES).transpose(0, 2, 1, 3)

    def through(carry, part, branch):
        return jnp.exp(-rates[branch] * part[branch, :, 16:]) * carry + part[branch, :, :16]

    totals = []
    for branch in range(2):
        order = range(grp) if branch == 0 else range(grp - 1, -1, -1)
        carry = jnp.zeros((width, 16, LANES), F32)
        for g in order:
            carry = through(carry, both[g], branch)
        span = jnp.sum(both[:, branch, :, 16:], axis=0)
        totals.append(jnp.concatenate([carry, span], 1))
    everything = lax.all_gather(jnp.stack(totals), "seq")
    carries = []
    for branch in range(2):
        carry = jnp.zeros((width, 16, LANES), F32)

        def turn(i, carry, branch=branch):
            at = i if branch == 0 else seq - 1 - i
            reached = at < here_s if branch == 0 else at > here_s
            return jnp.where(reached, through(carry, everything[at], branch), carry)

        carry = lax.fori_loop(0, seq, turn, carry)
        order = range(grp) if branch == 0 else range(grp - 1, -1, -1)
        each = [None] * grp
        for g in order:
            each[g] = carry
            carry = through(carry, both[g], branch)
        carries.append(jnp.stack(each))
    back = jnp.stack(carries, 1)
    back = lax.all_to_all(back, "grp", split_axis=0, concat_axis=0, tiled=True)
    return back.transpose(1, 0, 2, 3, 4).reshape(2, tiles, 16, LANES)


def local(
    inner_input,
    inner_gate,
    conv_weight,
    conv_bias,
    proj_weight,
    step_weight,
    step_bias,
    decay_rate,
    skip_gain,
):
    width = conv_weight.shape[2]
    small = jnp.concatenate(
        [
            conv_weight.reshape(8, width),
            conv_bias,
            step_bias,
            skip_gain,
            jnp.zeros((2, width), F32),
            decay_rate.reshape(32, width) * -LOG2E,
        ],
        0,
    )
    small = lax.all_gather(small, "grp")
    proj_weight = lax.all_gather(jnp.swapaxes(proj_weight, 1, 2), "grp")
    step_weight = lax.all_gather(step_weight, "grp")
    axes = ("seq", "grp")
    count = lax.axis_size("seq") * lax.axis_size("grp")
    before = lax.ppermute(inner_input[-16:], axes, [(i, i + 1) for i in range(count - 1)])
    after = lax.ppermute(inner_input[:16], axes, [(i + 1, i) for i in range(count - 1)])
    y, end, step, state, elapsed, out_half = run_front(
        inner_input, before, after, small, proj_weight, step_weight
    )
    carry = entering_states(state, elapsed[:, :, 0], decay_rate)
    return run_back(y, end, step, out_half, small, carry, inner_gate)


def solution(mesh):
    placed = (
        P(("seq", "grp"), None),
        P(("seq", "grp"), None),
        P(None, None, "grp"),
        P(None, "grp"),
        P(None, "grp", None),
        P(None, None, "grp"),
        P(None, "grp"),
        P(None, None, "grp"),
        P(None, "grp"),
    )
    return jax.shard_map(
        local, mesh=mesh, in_specs=placed, out_specs=P(("seq", "grp"), None), check_vma=False
    )
```

```python
import functools
import math

import jax
import jax.numpy as jnp
from jax import lax
from jax.experimental import pallas as pl
from jax.experimental.pallas import tpu as pltpu
from jax.sharding import PartitionSpec as P

F32 = jnp.float32
BF16 = jnp.bfloat16
LOG2E = math.log2(math.e)
LN2 = math.log(2.0)

CHUNKS = 8
LANES = 128

ROW_CONV = 0
ROW_BIAS = 8
ROW_STEP = 10
ROW_SKIP = 12
ROW_RATE = 16
ROWS_SMALL = 48
HALO = 16
MESH = pl.DeviceIdType.MESH


def iota(shape, dim):
    return lax.broadcasted_iota(jnp.int32, shape, dim)


def silu(value):
    half = 0.5 * value
    return half + half * jnp.tanh(half)


def softplus(value):
    small = jnp.exp2(jnp.abs(value) * -LOG2E)
    series = small * (1.0 - small * (0.5 - small * (1.0 / 3.0 - small * 0.25)))
    logarithm = LN2 * jnp.log2(1.0 + small)
    return jnp.maximum(value, 0.0) + jnp.where(small < 0.02, series, logarithm)


def dot_t(a, b):
    return lax.dot_general(a, b, (((1,), (1,)), ((), ())), preferred_element_type=F32)


def convolve(tile, rows_ref, first, last, small_ref, u_ref, rows_f32):
    rows = rows_ref.shape[0] - 2 * HALO
    steps = rows // CHUNKS
    shard, column = lax.div(tile, 4), lax.rem(tile, 4)
    cols = pl.ds(pl.multiple_of(tile * LANES, LANES), LANES)
    lanes = pl.ds(pl.multiple_of(column * LANES, LANES), LANES)
    rows_f32[0:HALO, :] = rows_ref[0:HALO, cols].astype(F32) * first
    rows_f32[HALO : HALO + rows, :] = rows_ref[HALO : HALO + rows, cols].astype(F32)
    rows_f32[HALO + rows : 2 * HALO + rows, :] = (
        rows_ref[HALO + rows : 2 * HALO + rows, cols].astype(F32) * last
    )
    taps = {t: rows_f32[pl.ds(HALO + t, CHUNKS, stride=steps), :] for t in range(-3, steps + 3)}
    for branch in range(2):
        weights = [
            jnp.broadcast_to(
                small_ref[shard, ROW_CONV + 4 * branch + j : ROW_CONV + 4 * branch + j + 1, lanes],
                (CHUNKS, LANES),
            )
            for j in range(4)
        ]
        bias = jnp.broadcast_to(
            small_ref[shard, ROW_BIAS + branch : ROW_BIAS + branch + 1, lanes], (CHUNKS, LANES)
        )
        sign = -1 if branch == 0 else 1
        for t in range(0, steps, 2):
            pair = []
            for s in (t, t + 1):
                total = bias
                for j in range(4):
                    total = total + weights[j] * taps[s + sign * (3 - j)]
                pair.append(silu(total))
            u_ref[branch, t * CHUNKS : (t + 2) * CHUNKS, cols] = jnp.concatenate(pair, 0).astype(
                BF16
            )


def spread_maps(branch, maps, in_wide, out_wide, out_half):
    rows = maps.shape[0]
    count = rows * 16
    r, c = iota((count, rows), 0), iota((count, rows), 1)
    pick = ((r >> 7) * CHUNKS + (r & 7) == c).astype(F32).astype(BF16)
    picked = jnp.dot(pick, maps, preferred_element_type=F32)
    r, c = iota((count, 32), 0), iota((count, 32), 1)
    state = (r >> 3) & 15
    ones = jnp.ones((32, LANES), BF16)
    in_wide[branch] = jnp.dot(
        jnp.where(state == c, picked, 0.0).astype(BF16), ones, preferred_element_type=F32
    )
    out_wide[branch] = jnp.dot(
        jnp.where(state + 16 == c, picked, 0.0).astype(BF16), ones, preferred_element_type=F32
    )
    r, c = iota((count, rows), 0), iota((count, rows), 1)
    pick = ((r >> 8) * 16 + (r & 15) == c).astype(F32).astype(BF16)
    picked = jnp.dot(pick, maps, preferred_element_type=F32)
    r, c = iota((count, 32), 0), iota((count, 32), 1)
    state = (r >> 4) & 15
    out_half[branch] = jnp.dot(
        jnp.where(state + 16 == c, picked, 0.0).astype(BF16), ones, preferred_element_type=F32
    ).astype(BF16)


def step_sizes(branch, shard, low, step_weight_ref, small_ref, step_ref):
    width = step_weight_ref.shape[-1]
    rows = low.shape[0]
    for q in range(width // LANES):
        lanes = slice(q * LANES, (q + 1) * LANES)
        value = jnp.dot(low, step_weight_ref[shard, branch, :, lanes], preferred_element_type=F32)
        value = value + small_ref[shard, ROW_STEP + branch : ROW_STEP + branch + 1, lanes]
        step_ref[branch, shard * (width // LANES) + q] = softplus(value).reshape(
            rows // CHUNKS, CHUNKS, LANES
        )


def scan_tile(
    branch, tile, u_ref, small_ref, step_ref, in_wide, out_wide, y_ref, end_ref, total_ref, fresh
):
    steps = step_ref.shape[2]
    shard, column = lax.div(tile, 4), lax.rem(tile, 4)
    cols = pl.ds(pl.multiple_of(tile * LANES, LANES), LANES)
    lanes = pl.ds(pl.multiple_of(column * LANES, LANES), LANES)
    first = ROW_RATE + 16 * branch
    skip = jnp.broadcast_to(
        small_ref[shard, ROW_SKIP + branch : ROW_SKIP + branch + 1, lanes], (CHUNKS, LANES)
    )
    for start in (0, 8):
        rates = jnp.stack(
            [
                jnp.broadcast_to(
                    small_ref[shard, first + n : first + n + 1, lanes], (CHUNKS, LANES)
                )
                for n in range(start, start + 8)
            ]
        )
        state = jnp.zeros((8, CHUNKS, LANES), F32)
        elapsed = jnp.zeros((CHUNKS, LANES), F32)
        for j in range(steps):
            t = j if branch == 0 else steps - 1 - j
            size = step_ref[branch, tile, t]
            u = u_ref[branch, pl.ds(t * CHUNKS, CHUNKS), cols].astype(F32)
            at = pl.ds((t * 16 + start) * CHUNKS, 8 * CHUNKS)
            into = in_wide[branch, at, :].reshape(8, CHUNKS, LANES)
            out = out_wide[branch, at, :].reshape(8, CHUNKS, LANES)
            state = jnp.exp2(rates * size[None]) * state + (size * u)[None] * into
            part = jnp.sum(out * state, axis=0)
            if start == 0:
                part = part + skip * u
                elapsed = elapsed + size
            if start > 0 or not fresh:
                part = part + y_ref[tile, t]
            y_ref[tile, t] = part
        if start == 0:
            total_ref[branch, tile] = elapsed
        end_ref[branch, tile, start * CHUNKS : (start + 8) * CHUNKS, :] = state.reshape(
            8 * CHUNKS, LANES
        )


def device_state(branch, tile, small_ref, end_ref, total_ref, message_ref):
    shard, column = lax.div(tile, 4), lax.rem(tile, 4)
    lanes = pl.ds(pl.multiple_of(column * LANES, LANES), LANES)
    first = ROW_RATE + 16 * branch
    rates = small_ref[shard, first : first + 16, lanes]
    state = jnp.zeros((16, LANES), F32)
    elapsed = jnp.zeros((1, LANES), F32)
    for j in range(CHUNKS):
        k = j if branch == 0 else CHUNKS - 1 - j
        span = total_ref[branch, tile, k : k + 1, :]
        state = jnp.exp2(rates * span) * state + end_ref[branch, tile, pl.ds(k, 16, stride=CHUNKS), :]
        elapsed = elapsed + span
    message_ref[branch, tile] = as_message(state, elapsed)


def as_message(state, elapsed):
    high = elapsed.astype(BF16).astype(F32)
    low = elapsed - high
    row = iota((16, LANES), 0)
    times = jnp.where(row == 0, high, jnp.where(row == 1, low, 0.0))
    return jnp.concatenate([state, times], 0).astype(BF16)


def of_message(message):
    values = message.astype(F32)
    return values[0:16], values[16:17] + values[17:18]


def correct_tile(
    branch, tile, small_ref, step_ref, end_ref, out_half, carry_ref, y_ref, total_ref, chunk_carry
):
    shard, column = lax.div(tile, 4), lax.rem(tile, 4)
    lanes = pl.ds(pl.multiple_of(column * LANES, LANES), LANES)
    first = ROW_RATE + 16 * branch
    steps = step_ref.shape[2]
    rates = small_ref[shard, first : first + 16, lanes]
    carry = carry_ref[branch, tile].astype(F32)
    for j in range(CHUNKS):
        k = j if branch == 0 else CHUNKS - 1 - j
        chunk_carry[pl.ds(k, 16, stride=CHUNKS), :] = carry
        if j < CHUNKS - 1:
            carry = (
                jnp.exp2(rates * total_ref[branch, tile, k : k + 1, :]) * carry
                + end_ref[branch, tile, pl.ds(k, 16, stride=CHUNKS), :]
            )
    entering = []
    wide = []
    for n in range(16):
        one = chunk_carry[n * CHUNKS : (n + 1) * CHUNKS, :]
        entering.append(jnp.concatenate([one, one], 0).astype(BF16))
        rate = small_ref[shard, first + n : first + n + 1, lanes]
        wide.append(jnp.broadcast_to(rate, (16, LANES)).astype(BF16))
    elapsed = jnp.zeros((CHUNKS, LANES), F32)
    for j in range(0, steps, 2):
        pair = []
        for i in (j, j + 1):
            t = i if branch == 0 else steps - 1 - i
            elapsed = elapsed + step_ref[branch, tile, t]
            pair.append(elapsed)
        low = j if branch == 0 else steps - 2 - j
        if branch == 1:
            pair = pair[::-1]
        spans = jnp.concatenate(pair, 0).astype(BF16)
        total = None
        for n in range(16):
            at = ((low // 2) * 16 + n) * 16
            part = jnp.exp2(wide[n] * spans) * entering[n] * out_half[branch, at : at + 16, :]
            total = part if total is None else total + part
        total = total.astype(F32)
        y_ref[tile, low] = y_ref[tile, low] + total[:CHUNKS]
        y_ref[tile, low + 1] = y_ref[tile, low + 1] + total[CHUNKS:]


def gate_tile(tile, y_ref, gate_ref, result_ref, rows_f32):
    steps = y_ref.shape[1]
    rows = gate_ref.shape[0]
    cols = pl.ds(pl.multiple_of(tile * LANES, LANES), LANES)
    for t in range(steps):
        rows_f32[pl.ds(t, CHUNKS, stride=steps), :] = y_ref[tile, t]
    mixed = rows_f32[0:rows, :].astype(BF16).astype(F32)
    result_ref[:, cols] = (mixed * silu(gate_ref[:, cols].astype(F32))).astype(BF16)


def whole_kernel(
    x_hbm, gate_hbm, small_own, proj_own, step_own, result_ref,
    rows_ref, gate_ref, small_ref, proj_weight_ref, step_weight_ref,
    u_ref, rows_f32, in_wide, out_wide, out_half, step_ref, y_ref, end_ref, total_ref, chunk_carry,
    out1, in1, out2, in2, out3, in3, local_state, local_time,
    local_sem, halo_send, halo_recv, gather_send, gather_recv,
    send1, recv1, send2, recv2, send3, recv3,
):
    s, g = lax.axis_index("seq"), lax.axis_index("grp")
    seq, grp = lax.axis_size("seq"), lax.axis_size("grp")
    y, core = lax.div(g, 2), lax.rem(g, 2)
    y_left, y_right, y_far = lax.rem(y + 3, 4), lax.rem(y + 1, 4), lax.rem(y + 2, 4)
    group, x = lax.div(s, 4), lax.rem(s, 4)
    member = x * grp + g
    members, groups = 4 * grp, seq // 4
    flip = 4 - 8 * lax.rem(group, 2)
    right = (s + lax.div(y + 1, 4) * flip, y_right * 2 + core)
    left = (s + (1 - lax.div(y + 3, 4)) * flip, y_left * 2 + core)
    sibling = (s, y * 2 + 1 - core)
    place = s * grp + g
    count = seq * grp
    after, before = lax.rem(place + 1, count), lax.rem(place + count - 1, count)
    after, before = (lax.div(after, grp), lax.rem(after, grp)), (lax.div(before, grp), lax.rem(before, grp))

    def member_at(k):
        return (group * 4 + lax.div(k, grp), lax.rem(k, grp))

    def group_at(k):
        return (k * 4 + x, g)

    barrier = pltpu.get_barrier_semaphore()

    def greet(device):
        pl.semaphore_signal(barrier, inc=1, device_id=device, device_id_type=MESH)

    for device in (right, left, after, before):
        greet(device)

    def greet_member(d, _):
        greet(member_at(lax.rem(member + d, members)))
        return 0

    def greet_group(d, _):
        greet(group_at(lax.rem(group + d, groups)))
        return 0

    lax.fori_loop(1, members, greet_member, 0)
    lax.fori_loop(1, groups, greet_group, 0)
    pl.semaphore_wait(barrier, 4 + members - 1 + groups - 1)

    def remote(src, dst, send, recv, device):
        return pltpu.make_async_remote_copy(
            src_ref=src, dst_ref=dst, send_sem=send, recv_sem=recv, device_id=device,
            device_id_type=MESH,
        )

    rows = x_hbm.shape[0]
    halos = [
        remote(x_hbm.at[rows - HALO : rows], rows_ref.at[0:HALO], halo_send.at[0], halo_recv.at[0], after),
        remote(
            x_hbm.at[0:HALO], rows_ref.at[HALO + rows : 2 * HALO + rows], halo_send.at[1],
            halo_recv.at[1], before,
        ),
    ]
    own = (small_own, proj_own, step_own)
    whole = (small_ref, proj_weight_ref, step_weight_ref)
    locals_ = [
        pltpu.make_async_copy(x_hbm, rows_ref.at[HALO : HALO + rows], local_sem.at[0]),
        pltpu.make_async_copy(gate_hbm, gate_ref, local_sem.at[1]),
    ] + [pltpu.make_async_copy(own[c], whole[c].at[g], local_sem.at[2 + c]) for c in range(3)]

    def part(kind, slot, half):
        if half is None:
            return whole[kind].at[slot]
        if kind == 0:
            return whole[kind].at[slot, half * (ROWS_SMALL // 2) : (half + 1) * (ROWS_SMALL // 2)]
        return whole[kind].at[slot, half]

    sent_slot = (g, g, y_left * 2 + core, y_right * 2 + core, g, y_left * 2 + core,
                 y_right * 2 + core, y_far * 2 + core, y_far * 2 + core)
    other = 1 - core
    got_slot = (y_left * 2 + core, y_right * 2 + core, y_far * 2 + core, y_far * 2 + core,
                y * 2 + other, y_left * 2 + other, y_right * 2 + other, y_far * 2 + other,
                y_far * 2 + other)
    halves = (None, None, 0, 1, None, None, None, 0, 1)
    targets = (right, left, right, left) + (sibling,) * 5

    def outgoing(kind, way):
        dst = part(kind, sent_slot[way], halves[way])
        src = own[kind] if way in (0, 1, 4) else dst
        return remote(src, dst, gather_send.at[kind, way], gather_recv.at[kind, way], targets[way])

    def arrived(kind, way):
        dst = part(kind, got_slot[way], halves[way])
        remote(dst, dst, gather_send.at[kind, way], gather_recv.at[kind, way], targets[way]).wait_recv()

    def send_own(kind):
        for way in (0, 1, 4):
            outgoing(kind, way).start()

    def forward_near(kind):
        arrived(kind, 0)
        outgoing(kind, 2).start()
        outgoing(kind, 5).start()
        arrived(kind, 1)
        outgoing(kind, 3).start()
        outgoing(kind, 6).start()

    def forward_far(kind):
        arrived(kind, 2)
        outgoing(kind, 7).start()
        arrived(kind, 3)
        outgoing(kind, 8).start()

    locals_[2].start()
    send_own(0)
    for copy in halos:
        copy.start()
    locals_[0].start()
    locals_[3].start()
    send_own(1)
    locals_[4].start()
    locals_[1].start()

    first = jnp.where(place == 0, 0.0, 1.0).astype(F32)
    last = jnp.where(place == count - 1, 0.0, 1.0).astype(F32)
    tiles_chip = 8

    def conv_chip(chip):
        def body(i, _):
            convolve(chip * tiles_chip + i, rows_ref, first, last, small_ref, u_ref, rows_f32)
            return 0

        lax.fori_loop(0, tiles_chip, body, 0)

    forward_near(0)
    locals_[0].wait()
    for copy in halos:
        copy.wait_recv()
    locals_[2].wait()
    arrived(0, 4)
    conv_chip(y)
    arrived(0, 5)
    conv_chip(y_left)
    forward_far(0)
    arrived(0, 6)
    conv_chip(y_right)
    arrived(0, 7)
    arrived(0, 8)
    conv_chip(y_far)

    width = proj_weight_ref.shape[-1]

    def project(chip, totals):
        new = []
        for branch in range(2):
            total = totals[branch]
            for i in range(2):
                shard = chip * 2 + i
                cols = pl.ds(pl.multiple_of(shard * width, width), width)
                total = total + dot_t(u_ref[branch, :, cols], proj_weight_ref[shard, branch])
            new.append(total)
        return new

    forward_near(1)
    send_own(2)
    locals_[3].wait()
    arrived(1, 4)
    totals = [jnp.zeros((rows, proj_weight_ref.shape[2]), F32)] * 2
    totals = project(y, totals)
    arrived(1, 5)
    totals = project(y_left, totals)
    forward_far(1)
    arrived(1, 6)
    totals = project(y_right, totals)
    arrived(1, 7)
    arrived(1, 8)
    totals = project(y_far, totals)
    lows = []
    for branch in range(2):
        projected = totals[branch].astype(BF16)
        spread_maps(branch, projected[:, 128:160], in_wide, out_wide, out_half)
        lows.append(projected[:, 0:128])

    def stage(branch, chip, fresh):
        for i in range(2):
            step_sizes(branch, chip * 2 + i, lows[branch], step_weight_ref, small_ref, step_ref)

        def body(i, _):
            scan_tile(
                branch, chip * tiles_chip + i, u_ref, small_ref, step_ref, in_wide, out_wide, y_ref,
                end_ref, total_ref, fresh,
            )
            return 0

        lax.fori_loop(0, tiles_chip, body, 0)

    tiles = 4 * tiles_chip

    def send_members(branch, source, target, send, recv):
        def body(d, _):
            k = lax.rem(member + d, members)
            remote(
                source.at[branch, k], target.at[branch, member], send.at[branch, d],
                recv.at[branch, d], member_at(k),
            ).start()
            return 0

        lax.fori_loop(1, members, body, 0)

    def await_members(branch, target, send, recv):
        def body(d, _):
            k = lax.rem(member + members - d, members)
            remote(
                target.at[branch, k], target.at[branch, k], send.at[branch, d], recv.at[branch, d],
                member_at(k),
            ).wait_recv()
            return 0

        lax.fori_loop(1, members, body, 0)

    def await_sent(branch, source, send, last):
        def body(d, _):
            remote(
                source, source, send.at[branch, d], send.at[branch, d], sibling
            ).wait_send()
            return 0

        lax.fori_loop(1, last, body, 0)

    def send_states(branch):
        def body(i, _):
            for q in range(4):
                device_state(branch, i * 4 + q, small_ref, end_ref, total_ref, out1)
            return 0

        lax.fori_loop(0, tiles // 4, body, 0)
        send_members(branch, out1, in1, send1, recv1)

    lanes = pl.ds(pl.multiple_of(lax.rem(member, 4) * LANES, LANES), LANES)

    def own_rates(branch):
        low = ROW_RATE + 16 * branch
        return small_ref[lax.div(member, 4), low : low + 16, lanes]

    def combine_members(branch):
        await_members(branch, in1, send1, recv1)
        in1[branch, member] = out1[branch, member]
        rates = own_rates(branch)
        state = jnp.zeros((16, LANES), F32)
        elapsed = jnp.zeros((1, LANES), F32)
        for j in range(members):
            k = j if branch == 0 else members - 1 - j
            local_state[branch, k] = state
            local_time[branch, k] = jnp.broadcast_to(elapsed, (8, LANES))
            gained, span = of_message(in1[branch, k])
            state = jnp.exp2(rates * span) * state + gained
            elapsed = elapsed + span
        out2[branch] = as_message(state, elapsed)

        def body(d, _):
            k = lax.rem(group + d, groups)
            remote(
                out2.at[branch], in2.at[branch, group], send2.at[branch, d], recv2.at[branch, d],
                group_at(k),
            ).start()
            return 0

        lax.fori_loop(1, groups, body, 0)

    def combine_groups(branch):
        def body(d, _):
            k = lax.rem(group + groups - d, groups)
            remote(
                in2.at[branch, k], in2.at[branch, k], send2.at[branch, d], recv2.at[branch, d],
                group_at(k),
            ).wait_recv()
            return 0

        lax.fori_loop(1, groups, body, 0)
        in2[branch, group] = out2[branch]
        rates = own_rates(branch)
        state = jnp.zeros((16, LANES), F32)
        for j in range(groups):
            k = j if branch == 0 else groups - 1 - j
            gained, span = of_message(in2[branch, k])
            new = jnp.exp2(rates * span) * state + gained
            state = jnp.where(k < group if branch == 0 else k > group, new, state)
        for k in range(members):
            out3[branch, k] = (
                jnp.exp2(rates * local_time[branch, k, 0:1, :]) * state + local_state[branch, k]
            ).astype(BF16)
        send_members(branch, out3, in3, send3, recv3)
        in3[branch, member] = out3[branch, member]

    def correct(branch, start, stop):
        def body(tile, _):
            correct_tile(
                branch, tile, small_ref, step_ref, end_ref, out_half, in3, y_ref, total_ref, chunk_carry
            )
            if branch == 1:
                gate_tile(tile, y_ref, gate_ref, result_ref, rows_f32)
            return 0

        lax.fori_loop(start, stop, body, 0)

    locals_[4].wait()
    arrived(2, 4)
    stage(0, y, True)
    forward_near(2)
    stage(1, y, False)
    arrived(2, 5)
    stage(0, y_left, True)
    forward_far(2)
    arrived(2, 6)
    stage(0, y_right, True)
    arrived(2, 7)
    arrived(2, 8)
    stage(0, y_far, True)
    send_states(0)
    stage(1, y_left, False)
    combine_members(0)
    stage(1, y_right, False)
    combine_groups(0)
    stage(1, y_far, False)
    send_states(1)
    await_members(0, in3, send3, recv3)
    correct(0, 0, tiles // 2)
    combine_members(1)
    correct(0, tiles // 2, tiles)
    combine_groups(1)
    locals_[1].wait()
    await_members(1, in3, send3, recv3)
    correct(1, 0, tiles)

    for copy in halos:
        copy.wait_send()
    for kind in range(3):
        for way in range(9):
            outgoing(kind, way).wait_send()
    for branch in range(2):
        await_sent(branch, out1.at[branch, 0], send1, members)
        await_sent(branch, out2.at[branch], send2, groups)
        await_sent(branch, out3.at[branch, 0], send3, members)


def run_whole(x, gate, small, proj_weight, step_weight):
    rows, channels = x.shape
    tiles, steps = channels // LANES, rows // CHUNKS
    shards = lax.axis_size("grp")
    members = 4 * shards
    groups = lax.axis_size("seq") // 4
    anywhere = pl.BlockSpec(memory_space=pl.ANY)
    vmem, dma = pltpu.VMEM, pltpu.SemaphoreType.DMA
    return pl.pallas_call(
        whole_kernel,
        out_shape=jax.ShapeDtypeStruct((rows, channels), BF16),
        in_specs=[anywhere] * 5,
        out_specs=pl.BlockSpec(memory_space=pltpu.VMEM),
        scratch_shapes=[
            vmem((rows + 2 * HALO, channels), BF16),
            vmem((rows, channels), BF16),
            vmem((shards,) + small.shape, F32),
            vmem((shards,) + proj_weight.shape, BF16),
            vmem((shards,) + step_weight.shape, BF16),
            vmem((2, rows, channels), BF16),
            vmem((rows + 2 * HALO, LANES), F32),
            vmem((2, rows * 16, LANES), F32),
            vmem((2, rows * 16, LANES), F32),
            vmem((2, rows * 16, LANES), BF16),
            vmem((2, tiles, steps, CHUNKS, LANES), F32),
            vmem((tiles, steps, CHUNKS, LANES), F32),
            vmem((2, tiles, 16 * CHUNKS, LANES), F32),
            vmem((2, tiles, CHUNKS, LANES), F32),
            vmem((16 * CHUNKS, LANES), F32),
            vmem((2, members, 32, LANES), BF16),
            vmem((2, members, 32, LANES), BF16),
            vmem((2, 32, LANES), BF16),
            vmem((2, groups, 32, LANES), BF16),
            vmem((2, members, 16, LANES), BF16),
            vmem((2, members, 16, LANES), BF16),
            vmem((2, members, 16, LANES), F32),
            vmem((2, members, 8, LANES), F32),
            dma((5,)),
            dma((2,)),
            dma((2,)),
            dma((3, 9)),
            dma((3, 9)),
            dma((2, members)),
            dma((2, members)),
            dma((2, groups)),
            dma((2, groups)),
            dma((2, members)),
            dma((2, members)),
        ],
        compiler_params=pltpu.CompilerParams(
            vmem_limit_bytes=56 << 20, collective_id=0, has_side_effects=True
        ),
    )(x, gate, small, proj_weight, step_weight)


def local(
    inner_input,
    inner_gate,
    conv_weight,
    conv_bias,
    proj_weight,
    step_weight,
    step_bias,
    decay_rate,
    skip_gain,
):
    width = conv_weight.shape[2]
    small = jnp.concatenate(
        [
            conv_weight.reshape(8, width),
            conv_bias,
            step_bias,
            skip_gain,
            jnp.zeros((2, width), F32),
            decay_rate.reshape(32, width) * -LOG2E,
        ],
        0,
    )
    return run_whole(inner_input, inner_gate, small, jnp.swapaxes(proj_weight, 1, 2), step_weight)


def solution(mesh):
    placed = (
        P(("seq", "grp"), None),
        P(("seq", "grp"), None),
        P(None, None, "grp"),
        P(None, "grp"),
        P(None, "grp", None),
        P(None, None, "grp"),
        P(None, "grp"),
        P(None, None, "grp"),
        P(None, "grp"),
    )
    return jax.shard_map(
        local, mesh=mesh, in_specs=placed, out_specs=P(("seq", "grp"), None), check_vma=False
    )
```

```python
import functools
import math

import jax
import jax.numpy as jnp
from jax import lax
from jax.experimental import pallas as pl
from jax.experimental.pallas import tpu as pltpu
from jax.sharding import PartitionSpec as P

F32 = jnp.float32
BF16 = jnp.bfloat16
LOG2E = math.log2(math.e)
LN2 = math.log(2.0)

CHUNKS = 8
LANES = 128

ROW_CONV = 0
ROW_BIAS = 8
ROWS_CONV = 16
ROW_STEP = 0
ROW_SKIP = 2
ROW_RATE = 8
ROWS_REST = 40
HALO = 16
MESH = pl.DeviceIdType.MESH


def iota(shape, dim):
    return lax.broadcasted_iota(jnp.int32, shape, dim)


def silu(value):
    half = 0.5 * value
    return half + half * jnp.tanh(half)


def softplus(value):
    small = jnp.exp2(jnp.abs(value) * -LOG2E)
    one_more = 1.0 + small
    return jnp.maximum(value, 0.0) + (LN2 * jnp.log2(one_more) + (small - (one_more - 1.0)))


def dot_t(a, b):
    return lax.dot_general(a, b, (((1,), (1,)), ((), ())), preferred_element_type=F32)


def convolve(tile, rows_ref, first, last, conv_ref, u_ref, rows_f32):
    rows = rows_ref.shape[0] - 2 * HALO
    steps = rows // CHUNKS
    shard, column = lax.div(tile, 4), lax.rem(tile, 4)
    cols = pl.ds(pl.multiple_of(tile * LANES, LANES), LANES)
    lanes = pl.ds(pl.multiple_of(column * LANES, LANES), LANES)
    rows_f32[0:HALO, :] = rows_ref[0:HALO, cols].astype(F32) * first
    rows_f32[HALO : HALO + rows, :] = rows_ref[HALO : HALO + rows, cols].astype(F32)
    rows_f32[HALO + rows : 2 * HALO + rows, :] = (
        rows_ref[HALO + rows : 2 * HALO + rows, cols].astype(F32) * last
    )
    taps = {t: rows_f32[pl.ds(HALO + t, CHUNKS, stride=steps), :] for t in range(-3, steps + 3)}
    for branch in range(2):
        weights = [
            jnp.broadcast_to(
                conv_ref[shard, ROW_CONV + 4 * branch + j : ROW_CONV + 4 * branch + j + 1, lanes],
                (CHUNKS, LANES),
            )
            for j in range(4)
        ]
        bias = jnp.broadcast_to(
            conv_ref[shard, ROW_BIAS + branch : ROW_BIAS + branch + 1, lanes], (CHUNKS, LANES)
        )
        sign = -1 if branch == 0 else 1
        for t in range(0, steps, 2):
            pair = []
            for s in (t, t + 1):
                total = bias
                for j in range(4):
                    total = total + weights[j] * taps[s + sign * (3 - j)]
                pair.append(silu(total))
            u_ref[branch, t * CHUNKS : (t + 2) * CHUNKS, cols] = jnp.concatenate(pair, 0).astype(
                BF16
            )


def spread_maps(branch, maps, in_wide, out_wide, out_half):
    rows = maps.shape[0]
    steps = rows // CHUNKS
    count = rows * 16
    tiles = maps.astype(F32).reshape(steps, 1, CHUNKS, 32)
    tiles = jnp.broadcast_to(tiles, (steps, 16, CHUNKS, 32)).reshape(count, 32)
    state = (iota((count, 32), 0) >> 3) & 15
    picked = jnp.where(state == (iota((count, 32), 1) & 15), tiles, 0.0).astype(BF16)
    ones = ((iota((32, 2 * LANES), 0) >> 4) == (iota((32, 2 * LANES), 1) >> 7)).astype(F32).astype(BF16)
    wide = jnp.dot(picked, ones, preferred_element_type=F32)
    in_wide[branch] = wide[:, :LANES]
    out_wide[branch] = wide[:, LANES:]
    pairs = wide[:, LANES:].reshape(steps // 2, 2, 16, CHUNKS, LANES)
    for pair in range(steps // 2):
        both = jnp.concatenate([pairs[pair, 0], pairs[pair, 1]], 1)
        out_half[branch, pair * 256 : (pair + 1) * 256, :] = both.reshape(256, LANES).astype(BF16)


def step_sizes(branch, shard, low, step_weight_ref, rest_ref, step_ref):
    width = step_weight_ref.shape[-1]
    rows = low.shape[0]
    value = jnp.dot(low, step_weight_ref[shard, branch], preferred_element_type=F32)
    value = softplus(value + rest_ref[shard, ROW_STEP + branch : ROW_STEP + branch + 1, :])
    for q in range(width // LANES):
        step_ref[branch, shard * (width // LANES) + q] = value[
            :, q * LANES : (q + 1) * LANES
        ].reshape(rows // CHUNKS, CHUNKS, LANES)


def scan_tile(
    branch, tile, u_ref, rest_ref, step_ref, in_wide, out_wide, y_ref, end_ref, total_ref, fresh
):
    steps = step_ref.shape[2]
    shard, column = lax.div(tile, 4), lax.rem(tile, 4)
    cols = pl.ds(pl.multiple_of(tile * LANES, LANES), LANES)
    lanes = pl.ds(pl.multiple_of(column * LANES, LANES), LANES)
    first = ROW_RATE + 16 * branch
    skip = jnp.broadcast_to(
        rest_ref[shard, ROW_SKIP + branch : ROW_SKIP + branch + 1, lanes], (CHUNKS, LANES)
    )
    for start in (0, 8):
        rates = jnp.stack(
            [
                jnp.broadcast_to(
                    rest_ref[shard, first + n : first + n + 1, lanes], (CHUNKS, LANES)
                )
                for n in range(start, start + 8)
            ]
        )
        state = jnp.zeros((8, CHUNKS, LANES), F32)
        elapsed = jnp.zeros((CHUNKS, LANES), F32)
        for j in range(steps):
            t = j if branch == 0 else steps - 1 - j
            size = step_ref[branch, tile, t]
            u = u_ref[branch, pl.ds(t * CHUNKS, CHUNKS), cols].astype(F32)
            at = pl.ds((t * 16 + start) * CHUNKS, 8 * CHUNKS)
            into = in_wide[branch, at, :].reshape(8, CHUNKS, LANES)
            out = out_wide[branch, at, :].reshape(8, CHUNKS, LANES)
            state = jnp.exp2(rates * size[None]) * state + (size * u)[None] * into
            part = jnp.sum(out * state, axis=0)
            if start == 0:
                part = part + skip * u
                elapsed = elapsed + size
            if start > 0 or not fresh:
                part = part + y_ref[tile, t]
            y_ref[tile, t] = part
        if start == 0:
            total_ref[branch, tile] = elapsed
        end_ref[branch, tile, start * CHUNKS : (start + 8) * CHUNKS, :] = state.reshape(
            8 * CHUNKS, LANES
        )


def device_state(branch, tile, rest_ref, end_ref, total_ref):
    shard, column = lax.div(tile, 4), lax.rem(tile, 4)
    lanes = pl.ds(pl.multiple_of(column * LANES, LANES), LANES)
    first = ROW_RATE + 16 * branch
    rates = rest_ref[shard, first : first + 16, lanes]
    state = jnp.zeros((16, LANES), F32)
    elapsed = jnp.zeros((1, LANES), F32)
    for j in range(CHUNKS):
        k = j if branch == 0 else CHUNKS - 1 - j
        span = total_ref[branch, tile, k : k + 1, :]
        state = jnp.exp2(rates * span) * state + end_ref[branch, tile, pl.ds(k, 16, stride=CHUNKS), :]
        elapsed = elapsed + span
    return state, elapsed


def as_message(state, elapsed):
    high = elapsed.astype(BF16).astype(F32)
    low = elapsed - high
    row = iota((16, LANES), 0)
    times = jnp.where(row == 0, high, jnp.where(row == 1, low, 0.0))
    return jnp.concatenate([state, times], 0).astype(BF16)


def of_message(message):
    values = message.astype(F32)
    return values[0:16], values[16:17] + values[17:18]


def correct_tile(
    branch, tile, rest_ref, step_ref, end_ref, out_half, carry, y_ref, total_ref, chunk_carry
):
    shard, column = lax.div(tile, 4), lax.rem(tile, 4)
    lanes = pl.ds(pl.multiple_of(column * LANES, LANES), LANES)
    first = ROW_RATE + 16 * branch
    steps = step_ref.shape[2]
    rates = rest_ref[shard, first : first + 16, lanes]
    for j in range(CHUNKS):
        k = j if branch == 0 else CHUNKS - 1 - j
        chunk_carry[pl.ds(k, 16, stride=CHUNKS), :] = carry
        if j < CHUNKS - 1:
            carry = (
                jnp.exp2(rates * total_ref[branch, tile, k : k + 1, :]) * carry
                + end_ref[branch, tile, pl.ds(k, 16, stride=CHUNKS), :]
            )
    entering = []
    wide = []
    for n in range(16):
        one = chunk_carry[n * CHUNKS : (n + 1) * CHUNKS, :]
        entering.append(jnp.concatenate([one, one], 0).astype(BF16))
        rate = rest_ref[shard, first + n : first + n + 1, lanes]
        wide.append(jnp.broadcast_to(rate, (16, LANES)).astype(BF16))
    elapsed = jnp.zeros((CHUNKS, LANES), F32)
    for j in range(0, steps, 2):
        pair = []
        for i in (j, j + 1):
            t = i if branch == 0 else steps - 1 - i
            elapsed = elapsed + step_ref[branch, tile, t]
            pair.append(elapsed)
        low = j if branch == 0 else steps - 2 - j
        if branch == 1:
            pair = pair[::-1]
        spans = jnp.concatenate(pair, 0).astype(BF16)
        total = None
        for n in range(16):
            at = ((low // 2) * 16 + n) * 16
            part = jnp.exp2(wide[n] * spans) * entering[n] * out_half[branch, at : at + 16, :]
            total = part if total is None else total + part
        total = total.astype(F32)
        y_ref[tile, low] = y_ref[tile, low] + total[:CHUNKS]
        y_ref[tile, low + 1] = y_ref[tile, low + 1] + total[CHUNKS:]


def mix_tile(tile, y_ref, result_ref, rows_f32):
    steps = y_ref.shape[1]
    rows = result_ref.shape[0]
    cols = pl.ds(pl.multiple_of(tile * LANES, LANES), LANES)
    for t in range(steps):
        rows_f32[pl.ds(t, CHUNKS, stride=steps), :] = y_ref[tile, t]
    result_ref[:, cols] = rows_f32[0:rows, :].astype(BF16)


def whole_kernel(
    x_hbm, conv_own, bias_own, proj_own, step_own, shift_own, rate_own, skip_own, result_ref,
    rows_ref, conv_in, bias_in, shift_in, rate_in, skip_in,
    conv_ref, proj_weight_ref, rest_ref, step_weight_ref,
    u_ref, rows_f32, in_wide, out_wide, out_half, step_ref, y_ref, end_ref, total_ref, chunk_carry,
    mine_state, mine_time, out0, in0, out1, in1, out2, in2, out3, in3, out4, in4, own_carry,
    local_state, local_time,
    local_sem, halo_send, halo_recv, gather_send, gather_recv,
    send0, recv0, send1, recv1, send2, recv2, send3, recv3, send4, recv4,
):
    s, g = lax.axis_index("seq"), lax.axis_index("grp")
    seq, grp = lax.axis_size("seq"), lax.axis_size("grp")
    y, core = lax.div(g, 2), lax.rem(g, 2)
    other = 1 - core
    y_left, y_right, y_far = lax.rem(y + 3, 4), lax.rem(y + 1, 4), lax.rem(y + 2, 4)
    group, x = lax.div(s, 4), lax.rem(s, 4)
    chip = x * 4 + y
    chips, groups = 16, seq // 4
    flip = 4 - 8 * lax.rem(group, 2)
    right = (s + lax.div(y + 1, 4) * flip, y_right * 2 + core)
    left = (s + (1 - lax.div(y + 3, 4)) * flip, y_left * 2 + core)
    sibling = (s, y * 2 + other)
    place = s * grp + g
    count = seq * grp
    after, before = lax.rem(place + 1, count), lax.rem(place + count - 1, count)
    after, before = (lax.div(after, grp), lax.rem(after, grp)), (lax.div(before, grp), lax.rem(before, grp))

    def chip_at(k):
        return (group * 4 + lax.div(k, 4), lax.rem(k, 4) * 2 + core)

    def group_at(k):
        return (k * 4 + x, g)

    def remote(src, dst, send, recv, device):
        return pltpu.make_async_remote_copy(
            src_ref=src, dst_ref=dst, send_sem=send, recv_sem=recv, device_id=device,
            device_id_type=MESH,
        )

    rows = x_hbm.shape[0]
    small_copies = [
        pltpu.make_async_copy(src, dst, local_sem.at[k])
        for k, (src, dst) in enumerate(
            [(conv_own, conv_in), (bias_own, bias_in), (shift_own, shift_in), (rate_own, rate_in),
             (skip_own, skip_in)]
        )
    ]
    rows_copy = pltpu.make_async_copy(x_hbm, rows_ref.at[HALO : HALO + rows], local_sem.at[5])
    proj_copy = pltpu.make_async_copy(proj_own, proj_weight_ref.at[g], local_sem.at[6])
    step_copy = pltpu.make_async_copy(step_own, step_weight_ref.at[g], local_sem.at[7])
    for copy in small_copies:
        copy.start()
    rows_copy.start()
    proj_copy.start()
    step_copy.start()

    barrier = pltpu.get_barrier_semaphore()

    def greet(device):
        pl.semaphore_signal(barrier, inc=1, device_id=device, device_id_type=MESH)

    for device in (right, left, after, before, sibling):
        greet(device)
    for d in range(1, chips):
        greet(chip_at(lax.rem(chip + d, chips)))
    for d in range(1, groups):
        greet(group_at(lax.rem(group + d, groups)))

    for copy in small_copies:
        copy.wait()
    width = conv_in.shape[-1]
    conv_ref[g, 0:4, :] = conv_in[0]
    conv_ref[g, 4:8, :] = conv_in[1]
    conv_ref[g, 8:10, :] = bias_in[...]
    conv_ref[g, 10:16, :] = jnp.zeros((6, width), F32)
    rest_ref[g, 0:2, :] = shift_in[...]
    rest_ref[g, 2:4, :] = skip_in[...]
    rest_ref[g, 4:8, :] = jnp.zeros((4, width), F32)
    rest_ref[g, 8:24, :] = rate_in[0] * -LOG2E
    rest_ref[g, 24:40, :] = rate_in[1] * -LOG2E
    pl.semaphore_wait(barrier, 5 + chips - 1 + groups - 1)

    halos = [
        remote(x_hbm.at[rows - HALO : rows], rows_ref.at[0:HALO], halo_send.at[0], halo_recv.at[0], after),
        remote(
            x_hbm.at[0:HALO], rows_ref.at[HALO + rows : 2 * HALO + rows], halo_send.at[1],
            halo_recv.at[1], before,
        ),
    ]
    whole = (conv_ref, proj_weight_ref, rest_ref, step_weight_ref)
    own = (conv_ref.at[g], proj_own, rest_ref.at[g], step_own)
    cuts = ((0, 8, 16), None, (0, 24, 40), None)

    def part(kind, slot, half):
        if half is None:
            return whole[kind].at[slot]
        if cuts[kind] is not None:
            return whole[kind].at[slot, cuts[kind][half] : cuts[kind][half + 1]]
        return whole[kind].at[slot, half]

    sent_slot = (g, g, y_left * 2 + core, y_right * 2 + core, g, y_left * 2 + core,
                 y_right * 2 + core, y_far * 2 + core, y_far * 2 + core)
    got_slot = (y_left * 2 + core, y_right * 2 + core, y_far * 2 + core, y_far * 2 + core,
                y * 2 + other, y_left * 2 + other, y_right * 2 + other, y_far * 2 + other,
                y_far * 2 + other)
    halves = (None, None, 0, 1, None, None, None, 0, 1)
    targets = (right, left, right, left) + (sibling,) * 5

    def outgoing(kind, way):
        dst = part(kind, sent_slot[way], halves[way])
        src = own[kind] if way in (0, 1, 4) else dst
        return remote(src, dst, gather_send.at[kind, way], gather_recv.at[kind, way], targets[way])

    def arrived(kind, way):
        dst = part(kind, got_slot[way], halves[way])
        remote(dst, dst, gather_send.at[kind, way], gather_recv.at[kind, way], targets[way]).wait_recv()

    def send_own(kind):
        for way in (0, 1, 4):
            outgoing(kind, way).start()

    def forward_near(kind):
        arrived(kind, 0)
        outgoing(kind, 2).start()
        outgoing(kind, 5).start()
        arrived(kind, 1)
        outgoing(kind, 3).start()
        outgoing(kind, 6).start()

    def forward_far(kind):
        arrived(kind, 2)
        outgoing(kind, 7).start()
        arrived(kind, 3)
        outgoing(kind, 8).start()

    send_own(0)
    for copy in halos:
        copy.start()
    send_own(1)

    first = jnp.where(place == 0, 0.0, 1.0).astype(F32)
    last = jnp.where(place == count - 1, 0.0, 1.0).astype(F32)
    tiles_chip = 8

    def conv_chip(at):
        def body(i, _):
            convolve(at * tiles_chip + i, rows_ref, first, last, conv_ref, u_ref, rows_f32.at[0])
            return 0

        lax.fori_loop(0, tiles_chip, body, 0)

    forward_near(0)
    rows_copy.wait()
    for copy in halos:
        copy.wait_recv()
    arrived(0, 4)
    conv_chip(y)
    arrived(0, 5)
    conv_chip(y_left)
    forward_far(0)
    arrived(0, 6)
    conv_chip(y_right)
    arrived(0, 7)
    arrived(0, 8)
    conv_chip(y_far)

    def project(at, totals):
        new = []
        for branch in range(2):
            total = totals[branch]
            for i in range(2):
                shard = at * 2 + i
                cols = pl.ds(pl.multiple_of(shard * width, width), width)
                total = total + dot_t(u_ref[branch, :, cols], proj_weight_ref[shard, branch])
            new.append(total)
        return new

    forward_near(1)
    send_own(2)
    send_own(3)
    proj_copy.wait()
    arrived(1, 4)
    totals = [jnp.zeros((rows, proj_weight_ref.shape[2]), F32)] * 2
    totals = project(y, totals)
    arrived(1, 5)
    totals = project(y_left, totals)
    forward_far(1)
    arrived(1, 6)
    totals = project(y_right, totals)
    arrived(1, 7)
    arrived(1, 8)
    totals = project(y_far, totals)
    lows = []
    for branch in range(2):
        projected = totals[branch].astype(BF16)
        spread_maps(branch, projected[:, 128:160], in_wide, out_wide, out_half)
        lows.append(projected[:, 0:128])

    def steps_of(branch, at):
        for i in range(2):
            step_sizes(branch, at * 2 + i, lows[branch], step_weight_ref, rest_ref, step_ref)

    def scan(branch, at):
        def body(i, _):
            scan_tile(
                branch, at * tiles_chip + i, u_ref, rest_ref, step_ref, in_wide, out_wide, y_ref,
                end_ref, total_ref, branch == 0,
            )
            return 0

        lax.fori_loop(0, tiles_chip, body, 0)

    def to_core(branch, at):
        span = pl.ds(at * 4, 4)
        return remote(
            out0.at[branch, span], in0.at[branch, span], send0.at[branch, at], recv0.at[branch, at],
            sibling,
        )

    def finish(branch, at):
        for i in range(4):
            k = at * 4 + i
            state, elapsed = device_state(branch, 2 * k + core, rest_ref, end_ref, total_ref)
            mine_state[branch, k] = state
            mine_time[branch, k] = jnp.broadcast_to(elapsed, (8, LANES))
            out0[branch, k] = as_message(
                *device_state(branch, 2 * k + other, rest_ref, end_ref, total_ref)
            )
        to_core(branch, at).start()

    def rates_of(branch, k):
        tile = 2 * k + core
        low = ROW_RATE + 16 * branch
        lanes = pl.ds(pl.multiple_of(lax.rem(tile, 4) * LANES, LANES), LANES)
        return rest_ref[lax.div(tile, 4), low : low + 16, lanes]

    def in_order(branch, k):
        here = (mine_state[branch, k], mine_time[branch, k, 0:1, :])
        there = of_message(in0[branch, k])
        leads = core == branch
        return [
            jnp.where(leads, a, b)
            for a, b in ((here[0], there[0]), (here[1], there[1]), (there[0], here[0]), (there[1], here[1]))
        ]

    def to_chip(branch, k):
        return remote(
            out1.at[branch, k], in1.at[branch, chip], send1.at[branch, k], recv1.at[branch, chip],
            chip_at(k),
        )

    def relay(branch, at):
        to_core(branch, at).wait_recv()
        for i in range(4):
            k = at * 4 + i
            state1, time1, state2, time2 = in_order(branch, k)
            state = jnp.exp2(rates_of(branch, k) * time2) * state1 + state2
            out1[branch, k] = as_message(state, time1 + time2)
        for i in range(4):
            k = at * 4 + i

            @pl.when(k != chip)
            def _():
                to_chip(branch, k).start()

    def combine_chips(branch):
        for d in range(1, chips):
            k = lax.rem(chip + chips - d, chips)
            remote(
                in1.at[branch, k], in1.at[branch, k], send1.at[branch, k], recv1.at[branch, k], chip_at(k)
            ).wait_recv()
        in1[branch, chip] = out1[branch, chip]
        rates = rates_of(branch, chip)
        state = jnp.zeros((16, LANES), F32)
        elapsed = jnp.zeros((1, LANES), F32)
        for j in range(chips):
            k = j if branch == 0 else chips - 1 - j
            local_state[branch, k] = state
            local_time[branch, k] = jnp.broadcast_to(elapsed, (8, LANES))
            gained, span = of_message(in1[branch, k])
            state = jnp.exp2(rates * span) * state + gained
            elapsed = elapsed + span
        out2[branch] = as_message(state, elapsed)
        for d in range(1, groups):
            k = lax.rem(group + d, groups)
            remote(
                out2.at[branch], in2.at[branch, group], send2.at[branch, k], recv2.at[branch, group],
                group_at(k),
            ).start()

    def combine_groups(branch):
        for d in range(1, groups):
            k = lax.rem(group + groups - d, groups)
            remote(
                in2.at[branch, k], in2.at[branch, k], send2.at[branch, k], recv2.at[branch, k], group_at(k)
            ).wait_recv()
        in2[branch, group] = out2[branch]
        rates = rates_of(branch, chip)
        state = jnp.zeros((16, LANES), F32)
        for j in range(groups):
            k = j if branch == 0 else groups - 1 - j
            gained, span = of_message(in2[branch, k])
            new = jnp.exp2(rates * span) * state + gained
            state = jnp.where(k < group if branch == 0 else k > group, new, state)
        for k in range(chips):
            out3[branch, k] = (
                jnp.exp2(rates * local_time[branch, k, 0:1, :]) * state + local_state[branch, k]
            ).astype(BF16)
        for d in range(1, chips):
            k = lax.rem(chip + d, chips)
            remote(
                out3.at[branch, k], in3.at[branch, chip], send3.at[branch, k], recv3.at[branch, chip],
                chip_at(k),
            ).start()

    def back_to_core(branch):
        return remote(out4.at[branch], in4.at[branch], send4.at[branch], recv4.at[branch], sibling)

    def receive(branch):
        for d in range(1, chips):
            k = lax.rem(chip + chips - d, chips)
            remote(
                in3.at[branch, k], in3.at[branch, k], send3.at[branch, k], recv3.at[branch, k], chip_at(k)
            ).wait_recv()
        in3[branch, chip] = out3[branch, chip]
        leads = core == branch
        for k in range(chips):
            carry = in3[branch, k].astype(F32)
            state1, time1, _, _ = in_order(branch, k)
            second = jnp.exp2(rates_of(branch, k) * time1) * carry + state1
            own_carry[branch, k] = jnp.where(leads, carry, second).astype(BF16)
            out4[branch, k] = jnp.where(leads, second, carry).astype(BF16)
        back_to_core(branch).start()

    def correct(branch, mine, start, stop):
        held = own_carry if mine else in4

        def body(i, _):
            for q in range(2):
                k = 2 * i + q
                tile = 2 * k + (core if mine else other)
                correct_tile(
                    branch, tile, rest_ref, step_ref, end_ref, out_half, held[branch, k].astype(F32),
                    y_ref, total_ref, chunk_carry.at[q],
                )
                if branch == 1:
                    mix_tile(tile, y_ref, result_ref, rows_f32.at[q])
            return 0

        lax.fori_loop(start // 2, stop // 2, body, 0)

    step_copy.wait()
    arrived(2, 4)
    arrived(3, 4)
    steps_of(0, y)
    scan(0, y)
    finish(0, y)
    forward_near(2)
    forward_near(3)
    steps_of(1, y)
    relay(0, y)
    scan(1, y)
    finish(1, y)
    arrived(2, 5)
    arrived(3, 5)
    steps_of(0, y_left)
    relay(1, y)
    scan(0, y_left)
    finish(0, y_left)
    forward_far(2)
    forward_far(3)
    arrived(2, 6)
    arrived(3, 6)
    steps_of(0, y_right)
    relay(0, y_left)
    scan(0, y_right)
    finish(0, y_right)
    for kind in (2, 3):
        for way in (7, 8):
            arrived(kind, way)
    steps_of(0, y_far)
    relay(0, y_right)
    scan(0, y_far)
    finish(0, y_far)
    steps_of(1, y_left)
    relay(0, y_far)
    scan(1, y_left)
    finish(1, y_left)
    combine_chips(0)
    steps_of(1, y_right)
    relay(1, y_left)
    scan(1, y_right)
    finish(1, y_right)
    combine_groups(0)
    steps_of(1, y_far)
    relay(1, y_right)
    scan(1, y_far)
    finish(1, y_far)
    receive(0)
    relay(1, y_far)
    correct(0, True, 0, 8)
    combine_chips(1)
    correct(0, True, 8, 16)
    back_to_core(0).wait_recv()
    correct(0, False, 0, 8)
    combine_groups(1)
    correct(0, False, 8, 16)
    receive(1)
    correct(1, True, 0, 16)
    back_to_core(1).wait_recv()
    correct(1, False, 0, 16)

    for copy in halos:
        copy.wait_send()
    for kind in range(4):
        for way in range(9):
            outgoing(kind, way).wait_send()
    for branch in range(2):
        for at in range(4):
            to_core(branch, at).wait_send()
        back_to_core(branch).wait_send()
        for d in range(1, chips):
            k = lax.rem(chip + d, chips)
            for source, send in ((out1, send1), (out3, send3)):
                remote(
                    source.at[branch, k], source.at[branch, k], send.at[branch, k], recv1.at[branch, k],
                    chip_at(k),
                ).wait_send()
        for d in range(1, groups):
            k = lax.rem(group + d, groups)
            remote(
                out2.at[branch], out2.at[branch], send2.at[branch, k], recv2.at[branch, k], group_at(k)
            ).wait_send()


def run_whole(x, conv_weight, conv_bias, proj_weight, step_weight, step_bias, decay_rate, skip_gain):
    rows, channels = x.shape
    width = conv_weight.shape[2]
    tiles, steps = channels // LANES, rows // CHUNKS
    shards = lax.axis_size("grp")
    chips = 2 * shards
    groups = lax.axis_size("seq") // 4
    anywhere = pl.BlockSpec(memory_space=pl.ANY)
    vmem, dma = pltpu.VMEM, pltpu.SemaphoreType.DMA
    return pl.pallas_call(
        whole_kernel,
        out_shape=jax.ShapeDtypeStruct((rows, channels), BF16),
        in_specs=[anywhere] * 8,
        out_specs=pl.BlockSpec(memory_space=pltpu.VMEM),
        scratch_shapes=[
            vmem((rows + 2 * HALO, channels), BF16),
            vmem(conv_weight.shape, F32),
            vmem(conv_bias.shape, F32),
            vmem(step_bias.shape, F32),
            vmem(decay_rate.shape, F32),
            vmem(skip_gain.shape, F32),
            vmem((shards, ROWS_CONV, width), F32),
            vmem((shards,) + proj_weight.shape, BF16),
            vmem((shards, ROWS_REST, width), F32),
            vmem((shards,) + step_weight.shape, BF16),
            vmem((2, rows, channels), BF16),
            vmem((2, rows + 2 * HALO, LANES), F32),
            vmem((2, rows * 16, LANES), F32),
            vmem((2, rows * 16, LANES), F32),
            vmem((2, rows * 16, LANES), BF16),
            vmem((2, tiles, steps, CHUNKS, LANES), F32),
            vmem((tiles, steps, CHUNKS, LANES), F32),
            vmem((2, tiles, 16 * CHUNKS, LANES), F32),
            vmem((2, tiles, CHUNKS, LANES), F32),
            vmem((2, 16 * CHUNKS, LANES), F32),
            vmem((2, chips, 16, LANES), F32),
            vmem((2, chips, 8, LANES), F32),
            vmem((2, chips, 32, LANES), BF16),
            vmem((2, chips, 32, LANES), BF16),
            vmem((2, chips, 32, LANES), BF16),
            vmem((2, chips, 32, LANES), BF16),
            vmem((2, 32, LANES), BF16),
            vmem((2, groups, 32, LANES), BF16),
            vmem((2, chips, 16, LANES), BF16),
            vmem((2, chips, 16, LANES), BF16),
            vmem((2, chips, 16, LANES), BF16),
            vmem((2, chips, 16, LANES), BF16),
            vmem((2, chips, 16, LANES), BF16),
            vmem((2, chips, 16, LANES), F32),
            vmem((2, chips, 8, LANES), F32),
            dma((8,)),
            dma((2,)),
            dma((2,)),
            dma((4, 9)),
            dma((4, 9)),
            dma((2, 4)),
            dma((2, 4)),
            dma((2, chips)),
            dma((2, chips)),
            dma((2, groups)),
            dma((2, groups)),
            dma((2, chips)),
            dma((2, chips)),
            dma((2,)),
            dma((2,)),
        ],
        compiler_params=pltpu.CompilerParams(
            vmem_limit_bytes=56 << 20, collective_id=0, has_side_effects=True
        ),
    )(x, conv_weight, conv_bias, proj_weight, step_weight, step_bias, decay_rate, skip_gain)


def local(
    inner_input,
    inner_gate,
    conv_weight,
    conv_bias,
    proj_weight,
    step_weight,
    step_bias,
    decay_rate,
    skip_gain,
):
    mixed = run_whole(
        inner_input, conv_weight, conv_bias, jnp.swapaxes(proj_weight, 1, 2), step_weight, step_bias,
        decay_rate, skip_gain,
    )
    return (mixed.astype(F32) * jax.nn.silu(inner_gate.astype(F32))).astype(BF16)


def solution(mesh):
    placed = (
        P(("seq", "grp"), None),
        P(("seq", "grp"), None),
        P(None, None, "grp"),
        P(None, "grp"),
        P(None, "grp", None),
        P(None, None, "grp"),
        P(None, "grp"),
        P(None, None, "grp"),
        P(None, "grp"),
    )
    return jax.shard_map(
        local, mesh=mesh, in_specs=placed, out_specs=P(("seq", "grp"), None), check_vma=False
    )
```

```python
import functools
import math

import jax
import jax.numpy as jnp
from jax import lax
from jax.experimental import pallas as pl
from jax.experimental.pallas import tpu as pltpu
from jax.sharding import PartitionSpec as P

F32 = jnp.float32
BF16 = jnp.bfloat16
LOG2E = math.log2(math.e)
LN2 = math.log(2.0)

CHUNKS = 8
LANES = 128

ROW_CONV = 0
ROW_BIAS = 8
ROWS_CONV = 16
ROW_STEP = 0
ROW_SKIP = 2
ROW_RATE = 8
ROWS_REST = 40
HALO = 16
DIRECT = (0, 1)
MESH = pl.DeviceIdType.MESH


def iota(shape, dim):
    return lax.broadcasted_iota(jnp.int32, shape, dim)


def silu(value):
    half = 0.5 * value
    return half + half * jnp.tanh(half)


def softplus(value):
    small = jnp.exp2(jnp.abs(value) * -LOG2E)
    one_more = 1.0 + small
    return jnp.maximum(value, 0.0) + (LN2 * jnp.log2(one_more) + (small - (one_more - 1.0)))


def dot_t(a, b):
    return lax.dot_general(a, b, (((1,), (1,)), ((), ())), preferred_element_type=F32)


def convolve(tile, rows_ref, first, last, conv_ref, u_ref, rows_f32):
    rows = rows_ref.shape[0] - 2 * HALO
    steps = rows // CHUNKS
    shard, column = lax.div(tile, 4), lax.rem(tile, 4)
    cols = pl.ds(pl.multiple_of(tile * LANES, LANES), LANES)
    lanes = pl.ds(pl.multiple_of(column * LANES, LANES), LANES)
    rows_f32[0:HALO, :] = rows_ref[0:HALO, cols].astype(F32) * first
    rows_f32[HALO : HALO + rows, :] = rows_ref[HALO : HALO + rows, cols].astype(F32)
    rows_f32[HALO + rows : 2 * HALO + rows, :] = (
        rows_ref[HALO + rows : 2 * HALO + rows, cols].astype(F32) * last
    )
    taps = {t: rows_f32[pl.ds(HALO + t, CHUNKS, stride=steps), :] for t in range(-3, steps + 3)}
    for branch in range(2):
        weights = [
            jnp.broadcast_to(
                conv_ref[shard, ROW_CONV + 4 * branch + j : ROW_CONV + 4 * branch + j + 1, lanes],
                (CHUNKS, LANES),
            )
            for j in range(4)
        ]
        bias = jnp.broadcast_to(
            conv_ref[shard, ROW_BIAS + branch : ROW_BIAS + branch + 1, lanes], (CHUNKS, LANES)
        )
        sign = -1 if branch == 0 else 1
        for t in range(0, steps, 2):
            pair = []
            for s in (t, t + 1):
                total = bias
                for j in range(4):
                    total = total + weights[j] * taps[s + sign * (3 - j)]
                pair.append(silu(total))
            u_ref[branch, t * CHUNKS : (t + 2) * CHUNKS, cols] = jnp.concatenate(pair, 0).astype(
                BF16
            )


def spread_maps(branch, maps, in_wide, out_wide, in_half, out_half):
    rows = maps.shape[0]
    steps = rows // CHUNKS
    count = rows * 16
    tiles = maps.astype(F32).reshape(steps, 1, CHUNKS, 32)
    tiles = jnp.broadcast_to(tiles, (steps, 16, CHUNKS, 32)).reshape(count, 32)
    state = (iota((count, 32), 0) >> 3) & 15
    picked = jnp.where(state == (iota((count, 32), 1) & 15), tiles, 0.0).astype(BF16)
    ones = ((iota((32, 2 * LANES), 0) >> 4) == (iota((32, 2 * LANES), 1) >> 7)).astype(F32).astype(BF16)
    wide = jnp.dot(picked, ones, preferred_element_type=F32)
    in_wide[branch] = wide[:, :LANES]
    out_wide[branch] = wide[:, LANES:]
    for half, target in ((0, in_half), (1, out_half)):
        pairs = wide[:, half * LANES : (half + 1) * LANES].reshape(steps // 2, 2, 16, CHUNKS, LANES)
        for pair in range(steps // 2):
            both = jnp.concatenate([pairs[pair, 0], pairs[pair, 1]], 1)
            target[branch, pair * 256 : (pair + 1) * 256, :] = both.reshape(256, LANES).astype(BF16)


def step_sizes(branch, shard, low, step_weight_ref, rest_ref, step_ref):
    width = step_weight_ref.shape[-1]
    rows = low.shape[0]
    value = jnp.dot(low, step_weight_ref[shard, branch], preferred_element_type=F32)
    value = softplus(value + rest_ref[shard, ROW_STEP + branch : ROW_STEP + branch + 1, :])
    for q in range(width // LANES):
        step_ref[branch, shard * (width // LANES) + q] = value[
            :, q * LANES : (q + 1) * LANES
        ].reshape(rows // CHUNKS, CHUNKS, LANES)


def scan_tile(
    branch, tile, u_ref, rest_ref, step_ref, in_wide, out_wide, y_ref, end_ref, total_ref, fresh
):
    steps = step_ref.shape[2]
    shard, column = lax.div(tile, 4), lax.rem(tile, 4)
    cols = pl.ds(pl.multiple_of(tile * LANES, LANES), LANES)
    lanes = pl.ds(pl.multiple_of(column * LANES, LANES), LANES)
    first = ROW_RATE + 16 * branch
    skip = jnp.broadcast_to(
        rest_ref[shard, ROW_SKIP + branch : ROW_SKIP + branch + 1, lanes], (CHUNKS, LANES)
    )
    for start in (0, 8):
        rates = jnp.stack(
            [
                jnp.broadcast_to(
                    rest_ref[shard, first + n : first + n + 1, lanes], (CHUNKS, LANES)
                )
                for n in range(start, start + 8)
            ]
        )
        state = jnp.zeros((8, CHUNKS, LANES), F32)
        elapsed = jnp.zeros((CHUNKS, LANES), F32)
        for j in range(steps):
            t = j if branch == 0 else steps - 1 - j
            size = step_ref[branch, tile, t]
            u = u_ref[branch, pl.ds(t * CHUNKS, CHUNKS), cols].astype(F32)
            at = pl.ds((t * 16 + start) * CHUNKS, 8 * CHUNKS)
            into = in_wide[branch, at, :].reshape(8, CHUNKS, LANES)
            out = out_wide[branch, at, :].reshape(8, CHUNKS, LANES)
            state = jnp.exp2(rates * size[None]) * state + (size * u)[None] * into
            part = jnp.sum(out * state, axis=0)
            if start == 0:
                part = part + skip * u
                elapsed = elapsed + size
            if start > 0 or not fresh:
                part = part + y_ref[tile, t]
            y_ref[tile, t] = part
        if start == 0 and fresh:
            total_ref[branch, tile] = elapsed
        end_ref[branch, tile, start * CHUNKS : (start + 8) * CHUNKS, :] = state.reshape(
            8 * CHUNKS, LANES
        )


def chunk_states(branch, tile, u_ref, rest_ref, step_ref, in_half, end_ref, total_ref):
    steps = step_ref.shape[2]
    shard, column = lax.div(tile, 4), lax.rem(tile, 4)
    cols = pl.ds(pl.multiple_of(tile * LANES, LANES), LANES)
    lanes = pl.ds(pl.multiple_of(column * LANES, LANES), LANES)
    first = ROW_RATE + 16 * branch
    rates = [
        jnp.broadcast_to(rest_ref[shard, first + n : first + n + 1, lanes], (16, LANES)).astype(BF16)
        for n in range(16)
    ]
    states = [None] * 16
    left = jnp.zeros((CHUNKS, LANES), F32)
    for j in range(0, steps, 2):
        pair, sizes = [], []
        for i in (j, j + 1):
            t = steps - 1 - i if branch == 0 else i
            size = step_ref[branch, tile, t]
            pair.append(left)
            sizes.append(size)
            left = left + size
        low = steps - 2 - j if branch == 0 else j
        if branch == 0:
            pair, sizes = pair[::-1], sizes[::-1]
        spans = jnp.concatenate(pair, 0).astype(BF16)
        drive = jnp.concatenate(sizes, 0).astype(BF16) * u_ref[branch, low * CHUNKS : (low + 2) * CHUNKS, cols]
        for n in range(16):
            at = ((low // 2) * 16 + n) * 16
            part = jnp.exp2(rates[n] * spans) * (drive * in_half[branch, at : at + 16, :])
            states[n] = part if states[n] is None else states[n] + part
    total_ref[branch, tile] = left
    for n in range(16):
        state = states[n].astype(F32)
        end_ref[branch, tile, n * CHUNKS : (n + 1) * CHUNKS, :] = state[:CHUNKS] + state[CHUNKS:]


def device_state(branch, tile, rest_ref, end_ref, total_ref):
    shard, column = lax.div(tile, 4), lax.rem(tile, 4)
    lanes = pl.ds(pl.multiple_of(column * LANES, LANES), LANES)
    first = ROW_RATE + 16 * branch
    rates = rest_ref[shard, first : first + 16, lanes]
    state = jnp.zeros((16, LANES), F32)
    elapsed = jnp.zeros((1, LANES), F32)
    for j in range(CHUNKS):
        k = j if branch == 0 else CHUNKS - 1 - j
        span = total_ref[branch, tile, k : k + 1, :]
        state = jnp.exp2(rates * span) * state + end_ref[branch, tile, pl.ds(k, 16, stride=CHUNKS), :]
        elapsed = elapsed + span
    return state, elapsed


def as_message(state, elapsed):
    high = elapsed.astype(BF16).astype(F32)
    low = elapsed - high
    row = iota((16, LANES), 0)
    times = jnp.where(row == 0, high, jnp.where(row == 1, low, 0.0))
    return jnp.concatenate([state, times], 0).astype(BF16)


def of_message(message):
    values = message.astype(F32)
    return values[0:16], values[16:17] + values[17:18]


def correct_tile(
    branch, tile, rest_ref, step_ref, end_ref, out_half, carry, y_ref, total_ref, chunk_carry
):
    shard, column = lax.div(tile, 4), lax.rem(tile, 4)
    lanes = pl.ds(pl.multiple_of(column * LANES, LANES), LANES)
    first = ROW_RATE + 16 * branch
    steps = step_ref.shape[2]
    rates = rest_ref[shard, first : first + 16, lanes]
    for j in range(CHUNKS):
        k = j if branch == 0 else CHUNKS - 1 - j
        chunk_carry[pl.ds(k, 16, stride=CHUNKS), :] = carry
        if j < CHUNKS - 1:
            carry = (
                jnp.exp2(rates * total_ref[branch, tile, k : k + 1, :]) * carry
                + end_ref[branch, tile, pl.ds(k, 16, stride=CHUNKS), :]
            )
    entering = []
    wide = []
    for n in range(16):
        one = chunk_carry[n * CHUNKS : (n + 1) * CHUNKS, :]
        entering.append(jnp.concatenate([one, one], 0).astype(BF16))
        rate = rest_ref[shard, first + n : first + n + 1, lanes]
        wide.append(jnp.broadcast_to(rate, (16, LANES)).astype(BF16))
    elapsed = jnp.zeros((CHUNKS, LANES), F32)
    for j in range(0, steps, 2):
        pair = []
        for i in (j, j + 1):
            t = i if branch == 0 else steps - 1 - i
            elapsed = elapsed + step_ref[branch, tile, t]
            pair.append(elapsed)
        low = j if branch == 0 else steps - 2 - j
        if branch == 1:
            pair = pair[::-1]
        spans = jnp.concatenate(pair, 0).astype(BF16)
        total = None
        for n in range(16):
            at = ((low // 2) * 16 + n) * 16
            part = jnp.exp2(wide[n] * spans) * entering[n] * out_half[branch, at : at + 16, :]
            total = part if total is None else total + part
        total = total.astype(F32)
        y_ref[tile, low] = y_ref[tile, low] + total[:CHUNKS]
        y_ref[tile, low + 1] = y_ref[tile, low + 1] + total[CHUNKS:]


def mix_tile(tile, y_ref, result_ref, rows_f32):
    steps = y_ref.shape[1]
    rows = result_ref.shape[0]
    cols = pl.ds(pl.multiple_of(tile * LANES, LANES), LANES)
    for t in range(steps):
        rows_f32[pl.ds(t, CHUNKS, stride=steps), :] = y_ref[tile, t]
    result_ref[:, cols] = rows_f32[0:rows, :].astype(BF16)


def whole_kernel(
    x_hbm, conv_own, bias_own, proj_own, step_own, shift_own, rate_own, skip_own, result_ref,
    rows_ref, conv_in, bias_in, shift_in, rate_in, skip_in,
    conv_ref, proj_weight_ref, rest_ref, step_weight_ref,
    u_ref, rows_f32, in_wide, out_wide, in_half, out_half, step_ref, y_ref, end_ref, total_ref, chunk_carry,
    mine_state, mine_time, out0, in0, out1, in1, out2, in2, out3, in3, out4, in4, own_carry,
    local_state, local_time,
    local_sem, halo_send, halo_recv, gather_send, gather_recv,
    send0, recv0, send1, recv1, send2, recv2, send3, recv3, send4, recv4,
):
    s, g = lax.axis_index("seq"), lax.axis_index("grp")
    seq, grp = lax.axis_size("seq"), lax.axis_size("grp")
    y, core = lax.div(g, 2), lax.rem(g, 2)
    other = 1 - core
    y_left, y_right, y_far = lax.rem(y + 3, 4), lax.rem(y + 1, 4), lax.rem(y + 2, 4)
    group, x = lax.div(s, 4), lax.rem(s, 4)
    chip = x * 4 + y
    chips, groups = 16, seq // 4
    flip = 4 - 8 * lax.rem(group, 2)
    right = (s + lax.div(y + 1, 4) * flip, y_right * 2 + core)
    left = (s + (1 - lax.div(y + 3, 4)) * flip, y_left * 2 + core)
    sibling = (s, y * 2 + other)
    right_far = (s + lax.div(y + 2, 4) * flip, y_far * 2 + core)
    left_far = (s + (1 - lax.div(y + 2, 4)) * flip, y_far * 2 + core)
    place = s * grp + g
    count = seq * grp
    after, before = lax.rem(place + 1, count), lax.rem(place + count - 1, count)
    after, before = (lax.div(after, grp), lax.rem(after, grp)), (lax.div(before, grp), lax.rem(before, grp))

    def chip_at(k):
        return (group * 4 + lax.div(k, 4), lax.rem(k, 4) * 2 + core)

    def group_at(k):
        return (k * 4 + x, g)

    def remote(src, dst, send, recv, device):
        return pltpu.make_async_remote_copy(
            src_ref=src, dst_ref=dst, send_sem=send, recv_sem=recv, device_id=device,
            device_id_type=MESH,
        )

    rows = x_hbm.shape[0]
    small_copies = [
        pltpu.make_async_copy(src, dst, local_sem.at[k])
        for k, (src, dst) in enumerate(
            [(conv_own, conv_in), (bias_own, bias_in), (shift_own, shift_in), (rate_own, rate_in),
             (skip_own, skip_in)]
        )
    ]
    rows_copy = pltpu.make_async_copy(x_hbm, rows_ref.at[HALO : HALO + rows], local_sem.at[5])
    proj_copy = pltpu.make_async_copy(proj_own, proj_weight_ref.at[g], local_sem.at[6])
    step_copy = pltpu.make_async_copy(step_own, step_weight_ref.at[g], local_sem.at[7])
    for copy in small_copies:
        copy.start()
    rows_copy.start()
    proj_copy.start()
    step_copy.start()

    barrier = pltpu.get_barrier_semaphore()

    def greet(device):
        pl.semaphore_signal(barrier, inc=1, device_id=device, device_id_type=MESH)

    for device in (right, left, right_far, left_far, after, before, sibling):
        greet(device)
    for d in range(1, chips):
        greet(chip_at(lax.rem(chip + d, chips)))
    for d in range(1, groups):
        greet(group_at(lax.rem(group + d, groups)))

    for copy in small_copies:
        copy.wait()
    width = conv_in.shape[-1]
    conv_ref[g, 0:4, :] = conv_in[0]
    conv_ref[g, 4:8, :] = conv_in[1]
    conv_ref[g, 8:10, :] = bias_in[...]
    conv_ref[g, 10:16, :] = jnp.zeros((6, width), F32)
    rest_ref[g, 0:2, :] = shift_in[...]
    rest_ref[g, 2:4, :] = skip_in[...]
    rest_ref[g, 4:8, :] = jnp.zeros((4, width), F32)
    rest_ref[g, 8:24, :] = rate_in[0] * -LOG2E
    rest_ref[g, 24:40, :] = rate_in[1] * -LOG2E
    pl.semaphore_wait(barrier, 7 + chips - 1 + groups - 1)

    halos = [
        remote(x_hbm.at[rows - HALO : rows], rows_ref.at[0:HALO], halo_send.at[0], halo_recv.at[0], after),
        remote(
            x_hbm.at[0:HALO], rows_ref.at[HALO + rows : 2 * HALO + rows], halo_send.at[1],
            halo_recv.at[1], before,
        ),
    ]
    whole = (conv_ref, proj_weight_ref, rest_ref, step_weight_ref, proj_weight_ref, step_weight_ref)
    own = (
        conv_ref.at[g], proj_own.at[0], rest_ref.at[g], step_own.at[0], proj_own.at[1], step_own.at[1]
    )
    branch_of = (None, 0, None, 0, 1, 1)
    cuts = ((0, 8, 16), (0, 80, 160), (0, 24, 40), (0, 64, 128), (0, 80, 160), (0, 64, 128))

    def part(kind, slot, half):
        low, high = (0, cuts[kind][2]) if half is None else cuts[kind][half : half + 2]
        if branch_of[kind] is None:
            return whole[kind].at[slot, low:high]
        return whole[kind].at[slot, branch_of[kind], low:high]

    sent_slot = (g, g, y_left * 2 + core, y_right * 2 + core, g, y_left * 2 + core,
                 y_right * 2 + core, y_far * 2 + core, y_far * 2 + core)
    got_slot = (y_left * 2 + core, y_right * 2 + core, y_far * 2 + core, y_far * 2 + core,
                y * 2 + other, y_left * 2 + other, y_right * 2 + other, y_far * 2 + other,
                y_far * 2 + other)
    halves = (None, None, 0, 1, None, None, None, 0, 1)
    targets = (right, left, right, left) + (sibling,) * 5

    def outgoing(kind, way):
        target = targets[way]
        if kind in DIRECT and way in (2, 3):
            dst = part(kind, g, halves[way])
            src = own_part(kind, halves[way])
            target = right_far if way == 2 else left_far
        else:
            dst = part(kind, sent_slot[way], halves[way])
            src = own[kind] if way in (0, 1, 4) else dst
        return remote(src, dst, gather_send.at[kind, way], gather_recv.at[kind, way], target)

    def arrived(kind, way):
        dst = part(kind, got_slot[way], halves[way])
        remote(dst, dst, gather_send.at[kind, way], gather_recv.at[kind, way], targets[way]).wait_recv()

    def own_part(kind, half):
        return own[kind].at[cuts[kind][half] : cuts[kind][half + 1]]

    def send_own(kind):
        for way in (0, 1, 2, 3, 4) if kind in DIRECT else (0, 1, 4):
            outgoing(kind, way).start()

    def forward_near(kind):
        for way in (0, 1):
            arrived(kind, way)
            if kind not in DIRECT:
                outgoing(kind, 2 + way).start()
            outgoing(kind, 5 + way).start()

    def forward_far(kind):
        arrived(kind, 2)
        outgoing(kind, 7).start()
        arrived(kind, 3)
        outgoing(kind, 8).start()

    send_own(0)
    for copy in halos:
        copy.start()
    send_own(1)

    first = jnp.where(place == 0, 0.0, 1.0).astype(F32)
    last = jnp.where(place == count - 1, 0.0, 1.0).astype(F32)
    tiles_chip = 8

    def conv_chip(at):
        def body(i, _):
            convolve(at * tiles_chip + i, rows_ref, first, last, conv_ref, u_ref, rows_f32.at[0])
            return 0

        lax.fori_loop(0, tiles_chip, body, 0)

    forward_near(0)
    rows_copy.wait()
    for copy in halos:
        copy.wait_recv()
    arrived(0, 4)
    conv_chip(y)
    arrived(0, 5)
    conv_chip(y_left)
    forward_far(0)
    arrived(0, 6)
    conv_chip(y_right)
    arrived(0, 7)
    arrived(0, 8)
    conv_chip(y_far)

    lows = [None, None]

    def project(branch, at, total):
        for i in range(2):
            shard = at * 2 + i
            cols = pl.ds(pl.multiple_of(shard * width, width), width)
            total = total + dot_t(u_ref[branch, :, cols], proj_weight_ref[shard, branch])
        return total

    def project_all(branch, kind):
        arrived(kind, 4)
        total = project(branch, y, jnp.zeros((rows, proj_weight_ref.shape[2]), F32))
        arrived(kind, 5)
        total = project(branch, y_left, total)
        if kind == 1:
            forward_far(kind)
        arrived(kind, 6)
        total = project(branch, y_right, total)
        arrived(kind, 7)
        arrived(kind, 8)
        projected = project(branch, y_far, total).astype(BF16)
        spread_maps(branch, projected[:, 128:160], in_wide, out_wide, in_half, out_half)
        lows[branch] = projected[:, 0:128]

    def steps_of(branch, at):
        for i in range(2):
            step_sizes(branch, at * 2 + i, lows[branch], step_weight_ref, rest_ref, step_ref)

    def scan(branch, at, start=0, stop=tiles_chip):
        def body(i, _):
            scan_tile(
                branch, at * tiles_chip + i, u_ref, rest_ref, step_ref, in_wide, out_wide, y_ref,
                end_ref, total_ref, branch == 0,
            )
            return 0

        lax.fori_loop(start, stop, body, 0)

    def states_of(branch, at):
        def body(i, _):
            chunk_states(
                branch, at * tiles_chip + i, u_ref, rest_ref, step_ref, in_half, end_ref, total_ref
            )
            return 0

        lax.fori_loop(0, tiles_chip, body, 0)

    def to_core(branch, at):
        span = pl.ds(at * 4, 4)
        return remote(
            out0.at[branch, span], in0.at[branch, span], send0.at[branch, at], recv0.at[branch, at],
            sibling,
        )

    def finish(branch, at):
        for i in range(4):
            k = at * 4 + i
            state, elapsed = device_state(branch, 2 * k + core, rest_ref, end_ref, total_ref)
            mine_state[branch, k] = state
            mine_time[branch, k] = jnp.broadcast_to(elapsed, (8, LANES))
            out0[branch, k] = as_message(
                *device_state(branch, 2 * k + other, rest_ref, end_ref, total_ref)
            )
        to_core(branch, at).start()

    def rates_of(branch, k):
        tile = 2 * k + core
        low = ROW_RATE + 16 * branch
        lanes = pl.ds(pl.multiple_of(lax.rem(tile, 4) * LANES, LANES), LANES)
        return rest_ref[lax.div(tile, 4), low : low + 16, lanes]

    def in_order(branch, k):
        here = (mine_state[branch, k], mine_time[branch, k, 0:1, :])
        there = of_message(in0[branch, k])
        leads = core == branch
        return [
            jnp.where(leads, a, b)
            for a, b in ((here[0], there[0]), (here[1], there[1]), (there[0], here[0]), (there[1], here[1]))
        ]

    def to_chip(branch, k):
        return remote(
            out1.at[branch, k], in1.at[branch, chip], send1.at[branch, k], recv1.at[branch, chip],
            chip_at(k),
        )

    def relay(branch, at):
        to_core(branch, at).wait_recv()
        for i in range(4):
            k = at * 4 + i
            state1, time1, state2, time2 = in_order(branch, k)
            state = jnp.exp2(rates_of(branch, k) * time2) * state1 + state2
            out1[branch, k] = as_message(state, time1 + time2)
        for i in range(4):
            k = at * 4 + i

            @pl.when(k != chip)
            def _():
                to_chip(branch, k).start()

    def combine_chips(branch):
        for d in range(1, chips):
            k = lax.rem(chip + chips - d, chips)
            remote(
                in1.at[branch, k], in1.at[branch, k], send1.at[branch, k], recv1.at[branch, k], chip_at(k)
            ).wait_recv()
        in1[branch, chip] = out1[branch, chip]
        rates = rates_of(branch, chip)
        state = jnp.zeros((16, LANES), F32)
        elapsed = jnp.zeros((1, LANES), F32)
        for j in range(chips):
            k = j if branch == 0 else chips - 1 - j
            local_state[branch, k] = state
            local_time[branch, k] = jnp.broadcast_to(elapsed, (8, LANES))
            gained, span = of_message(in1[branch, k])
            state = jnp.exp2(rates * span) * state + gained
            elapsed = elapsed + span
        out2[branch] = as_message(state, elapsed)
        for d in range(1, groups):
            k = lax.rem(group + d, groups)
            remote(
                out2.at[branch], in2.at[branch, group], send2.at[branch, k], recv2.at[branch, group],
                group_at(k),
            ).start()

    def combine_groups(branch):
        for d in range(1, groups):
            k = lax.rem(group + groups - d, groups)
            remote(
                in2.at[branch, k], in2.at[branch, k], send2.at[branch, k], recv2.at[branch, k], group_at(k)
            ).wait_recv()
        in2[branch, group] = out2[branch]
        rates = rates_of(branch, chip)
        state = jnp.zeros((16, LANES), F32)
        for j in range(groups):
            k = j if branch == 0 else groups - 1 - j
            gained, span = of_message(in2[branch, k])
            new = jnp.exp2(rates * span) * state + gained
            state = jnp.where(k < group if branch == 0 else k > group, new, state)
        for k in range(chips):
            out3[branch, k] = (
                jnp.exp2(rates * local_time[branch, k, 0:1, :]) * state + local_state[branch, k]
            ).astype(BF16)
        for d in range(1, chips):
            k = lax.rem(chip + d, chips)
            remote(
                out3.at[branch, k], in3.at[branch, chip], send3.at[branch, k], recv3.at[branch, chip],
                chip_at(k),
            ).start()

    def back_to_core(branch):
        return remote(out4.at[branch], in4.at[branch], send4.at[branch], recv4.at[branch], sibling)

    def receive(branch):
        for d in range(1, chips):
            k = lax.rem(chip + chips - d, chips)
            remote(
                in3.at[branch, k], in3.at[branch, k], send3.at[branch, k], recv3.at[branch, k], chip_at(k)
            ).wait_recv()
        in3[branch, chip] = out3[branch, chip]
        leads = core == branch
        for k in range(chips):
            carry = in3[branch, k].astype(F32)
            state1, time1, _, _ = in_order(branch, k)
            second = jnp.exp2(rates_of(branch, k) * time1) * carry + state1
            own_carry[branch, k] = jnp.where(leads, carry, second).astype(BF16)
            out4[branch, k] = jnp.where(leads, second, carry).astype(BF16)
        back_to_core(branch).start()

    def correct(branch, mine, start, stop):
        held = own_carry if mine else in4

        def body(i, _):
            for q in range(2):
                k = 2 * i + q
                tile = 2 * k + (core if mine else other)
                correct_tile(
                    branch, tile, rest_ref, step_ref, end_ref, out_half, held[branch, k].astype(F32),
                    y_ref, total_ref, chunk_carry.at[q],
                )
                if branch == 1:
                    mix_tile(tile, y_ref, result_ref, rows_f32.at[q])
            return 0

        lax.fori_loop(start // 2, stop // 2, body, 0)

    forward_near(1)
    send_own(2)
    send_own(3)
    proj_copy.wait()
    project_all(0, 1)

    step_copy.wait()
    arrived(2, 4)
    arrived(3, 4)
    steps_of(0, y)
    forward_near(2)
    forward_near(3)
    send_own(4)
    send_own(5)
    scan(0, y)
    finish(0, y)
    arrived(2, 5)
    arrived(3, 5)
    steps_of(0, y_left)
    forward_far(2)
    forward_far(3)
    relay(0, y)
    scan(0, y_left)
    finish(0, y_left)
    arrived(2, 6)
    arrived(3, 6)
    steps_of(0, y_right)
    relay(0, y_left)
    scan(0, y_right, 0, 4)
    forward_near(4)
    scan(0, y_right, 4, 8)
    finish(0, y_right)
    for kind in (2, 3):
        for way in (7, 8):
            arrived(kind, way)
    steps_of(0, y_far)
    relay(0, y_right)
    scan(0, y_far, 0, 4)
    forward_near(5)
    forward_far(4)
    scan(0, y_far, 4, 8)
    finish(0, y_far)
    project_all(1, 4)
    relay(0, y_far)
    arrived(5, 4)
    steps_of(1, y)
    forward_far(5)
    states_of(1, y)
    finish(1, y)
    arrived(5, 5)
    steps_of(1, y_left)
    relay(1, y)
    states_of(1, y_left)
    finish(1, y_left)
    arrived(5, 6)
    steps_of(1, y_right)
    relay(1, y_left)
    states_of(1, y_right)
    finish(1, y_right)
    combine_chips(0)
    arrived(5, 7)
    arrived(5, 8)
    steps_of(1, y_far)
    relay(1, y_right)
    states_of(1, y_far)
    finish(1, y_far)
    scan(1, y, 0, 4)
    relay(1, y_far)
    scan(1, y, 4, 8)
    scan(1, y_left)
    combine_groups(0)
    scan(1, y_right, 0, 4)
    combine_chips(1)
    scan(1, y_right, 4, 8)
    scan(1, y_far)
    receive(0)
    correct(0, True, 0, 16)
    combine_groups(1)
    back_to_core(0).wait_recv()
    correct(0, False, 0, 16)
    receive(1)
    correct(1, True, 0, 16)
    back_to_core(1).wait_recv()
    correct(1, False, 0, 16)

    for copy in halos:
        copy.wait_send()
    for kind in range(6):
        for way in range(9):
            outgoing(kind, way).wait_send()
    for branch in range(2):
        for at in range(4):
            to_core(branch, at).wait_send()
        back_to_core(branch).wait_send()
        for d in range(1, chips):
            k = lax.rem(chip + d, chips)
            for source, send in ((out1, send1), (out3, send3)):
                remote(
                    source.at[branch, k], source.at[branch, k], send.at[branch, k], recv1.at[branch, k],
                    chip_at(k),
                ).wait_send()
        for d in range(1, groups):
            k = lax.rem(group + d, groups)
            remote(
                out2.at[branch], out2.at[branch], send2.at[branch, k], recv2.at[branch, k], group_at(k)
            ).wait_send()


def run_whole(x, conv_weight, conv_bias, proj_weight, step_weight, step_bias, decay_rate, skip_gain):
    rows, channels = x.shape
    width = conv_weight.shape[2]
    tiles, steps = channels // LANES, rows // CHUNKS
    shards = lax.axis_size("grp")
    chips = 2 * shards
    groups = lax.axis_size("seq") // 4
    anywhere = pl.BlockSpec(memory_space=pl.ANY)
    vmem, dma = pltpu.VMEM, pltpu.SemaphoreType.DMA
    return pl.pallas_call(
        whole_kernel,
        out_shape=jax.ShapeDtypeStruct((rows, channels), BF16),
        in_specs=[anywhere] * 8,
        out_specs=pl.BlockSpec(memory_space=pltpu.VMEM),
        scratch_shapes=[
            vmem((rows + 2 * HALO, channels), BF16),
            vmem(conv_weight.shape, F32),
            vmem(conv_bias.shape, F32),
            vmem(step_bias.shape, F32),
            vmem(decay_rate.shape, F32),
            vmem(skip_gain.shape, F32),
            vmem((shards, ROWS_CONV, width), F32),
            vmem((shards,) + proj_weight.shape, BF16),
            vmem((shards, ROWS_REST, width), F32),
            vmem((shards,) + step_weight.shape, BF16),
            vmem((2, rows, channels), BF16),
            vmem((2, rows + 2 * HALO, LANES), F32),
            vmem((2, rows * 16, LANES), F32),
            vmem((2, rows * 16, LANES), F32),
            vmem((2, rows * 16, LANES), BF16),
            vmem((2, rows * 16, LANES), BF16),
            vmem((2, tiles, steps, CHUNKS, LANES), F32),
            vmem((tiles, steps, CHUNKS, LANES), F32),
            vmem((2, tiles, 16 * CHUNKS, LANES), F32),
            vmem((2, tiles, CHUNKS, LANES), F32),
            vmem((2, 16 * CHUNKS, LANES), F32),
            vmem((2, chips, 16, LANES), F32),
            vmem((2, chips, 8, LANES), F32),
            vmem((2, chips, 32, LANES), BF16),
            vmem((2, chips, 32, LANES), BF16),
            vmem((2, chips, 32, LANES), BF16),
            vmem((2, chips, 32, LANES), BF16),
            vmem((2, 32, LANES), BF16),
            vmem((2, groups, 32, LANES), BF16),
            vmem((2, chips, 16, LANES), BF16),
            vmem((2, chips, 16, LANES), BF16),
            vmem((2, chips, 16, LANES), BF16),
            vmem((2, chips, 16, LANES), BF16),
            vmem((2, chips, 16, LANES), BF16),
            vmem((2, chips, 16, LANES), F32),
            vmem((2, chips, 8, LANES), F32),
            dma((8,)),
            dma((2,)),
            dma((2,)),
            dma((6, 9)),
            dma((6, 9)),
            dma((2, 4)),
            dma((2, 4)),
            dma((2, chips)),
            dma((2, chips)),
            dma((2, groups)),
            dma((2, groups)),
            dma((2, chips)),
            dma((2, chips)),
            dma((2,)),
            dma((2,)),
        ],
        compiler_params=pltpu.CompilerParams(
            vmem_limit_bytes=56 << 20, collective_id=0, has_side_effects=True
        ),
    )(x, conv_weight, conv_bias, proj_weight, step_weight, step_bias, decay_rate, skip_gain)


def local(
    inner_input,
    inner_gate,
    conv_weight,
    conv_bias,
    proj_weight,
    step_weight,
    step_bias,
    decay_rate,
    skip_gain,
):
    mixed = run_whole(
        inner_input, conv_weight, conv_bias, jnp.swapaxes(proj_weight, 1, 2), step_weight, step_bias,
        decay_rate, skip_gain,
    )
    return (mixed.astype(F32) * jax.nn.silu(inner_gate.astype(F32))).astype(BF16)


def solution(mesh):
    placed = (
        P(("seq", "grp"), None),
        P(("seq", "grp"), None),
        P(None, None, "grp"),
        P(None, "grp"),
        P(None, "grp", None),
        P(None, None, "grp"),
        P(None, "grp"),
        P(None, None, "grp"),
        P(None, "grp"),
    )
    return jax.shard_map(
        local, mesh=mesh, in_specs=placed, out_specs=P(("seq", "grp"), None), check_vma=False
    )
```

```python
import functools
import math

import jax
import jax.numpy as jnp
from jax import lax
from jax.experimental import pallas as pl
from jax.experimental.pallas import tpu as pltpu
from jax.sharding import PartitionSpec as P

F32 = jnp.float32
BF16 = jnp.bfloat16
LOG2E = math.log2(math.e)
LN2 = math.log(2.0)

CHUNKS = 8
LANES = 128

ROW_CONV = 0
ROW_BIAS = 8
ROWS_CONV = 16
ROW_STEP = 0
ROW_SKIP = 2
ROW_RATE = 8
ROWS_REST = 40
HALO = 16
DIRECT = (0, 1)
MESH = pl.DeviceIdType.MESH


def iota(shape, dim):
    return lax.broadcasted_iota(jnp.int32, shape, dim)


def silu(value):
    half = 0.5 * value
    return half + half * jnp.tanh(half)


def softplus(value):
    small = jnp.exp2(jnp.abs(value) * -LOG2E)
    one_more = 1.0 + small
    return jnp.maximum(value, 0.0) + (LN2 * jnp.log2(one_more) + (small - (one_more - 1.0)))


def dot_t(a, b):
    return lax.dot_general(a, b, (((1,), (1,)), ((), ())), preferred_element_type=F32)


def convolve(tile, rows_ref, first, last, conv_ref, u_ref, rows_f32):
    rows = rows_ref.shape[0] - 2 * HALO
    steps = rows // CHUNKS
    shard, column = lax.div(tile, 4), lax.rem(tile, 4)
    cols = pl.ds(pl.multiple_of(tile * LANES, LANES), LANES)
    lanes = pl.ds(pl.multiple_of(column * LANES, LANES), LANES)
    rows_f32[0:HALO, :] = rows_ref[0:HALO, cols].astype(F32) * first
    rows_f32[HALO : HALO + rows, :] = rows_ref[HALO : HALO + rows, cols].astype(F32)
    rows_f32[HALO + rows : 2 * HALO + rows, :] = (
        rows_ref[HALO + rows : 2 * HALO + rows, cols].astype(F32) * last
    )
    taps = {t: rows_f32[pl.ds(HALO + t, CHUNKS, stride=steps), :] for t in range(-3, steps + 3)}
    for branch in range(2):
        weights = [
            jnp.broadcast_to(
                conv_ref[shard, ROW_CONV + 4 * branch + j : ROW_CONV + 4 * branch + j + 1, lanes],
                (CHUNKS, LANES),
            )
            for j in range(4)
        ]
        bias = jnp.broadcast_to(
            conv_ref[shard, ROW_BIAS + branch : ROW_BIAS + branch + 1, lanes], (CHUNKS, LANES)
        )
        sign = -1 if branch == 0 else 1
        for t in range(0, steps, 2):
            pair = []
            for s in (t, t + 1):
                total = bias
                for j in range(4):
                    total = total + weights[j] * taps[s + sign * (3 - j)]
                pair.append(silu(total))
            u_ref[branch, t * CHUNKS : (t + 2) * CHUNKS, cols] = jnp.concatenate(pair, 0).astype(
                BF16
            )


def spread_maps(branch, maps, in_wide, out_wide, in_half, out_half):
    rows = maps.shape[0]
    steps = rows // CHUNKS
    count = rows * 16
    tiles = maps.astype(F32).reshape(steps, 1, CHUNKS, 32)
    tiles = jnp.broadcast_to(tiles, (steps, 16, CHUNKS, 32)).reshape(count, 32)
    state = (iota((count, 32), 0) >> 3) & 15
    picked = jnp.where(state == (iota((count, 32), 1) & 15), tiles, 0.0).astype(BF16)
    ones = ((iota((32, 2 * LANES), 0) >> 4) == (iota((32, 2 * LANES), 1) >> 7)).astype(F32).astype(BF16)
    wide = jnp.dot(picked, ones, preferred_element_type=F32)
    in_wide[branch] = wide[:, :LANES]
    out_wide[branch] = wide[:, LANES:]
    for half, target in ((0, in_half), (1, out_half)):
        pairs = wide[:, half * LANES : (half + 1) * LANES].reshape(steps // 2, 2, 16, CHUNKS, LANES)
        for pair in range(steps // 2):
            both = jnp.concatenate([pairs[pair, 0], pairs[pair, 1]], 1)
            target[branch, pair * 256 : (pair + 1) * 256, :] = both.reshape(256, LANES).astype(BF16)


def step_sizes(branch, shard, low, step_weight_ref, rest_ref, step_ref):
    width = step_weight_ref.shape[-1]
    rows = low.shape[0]
    value = jnp.dot(low, step_weight_ref[shard, branch], preferred_element_type=F32)
    value = softplus(value + rest_ref[shard, ROW_STEP + branch : ROW_STEP + branch + 1, :])
    for q in range(width // LANES):
        step_ref[branch, shard * (width // LANES) + q] = value[
            :, q * LANES : (q + 1) * LANES
        ].reshape(rows // CHUNKS, CHUNKS, LANES)


def scan_tile(
    branch, tile, u_ref, rest_ref, step_ref, in_wide, out_wide, y_ref, end_ref, total_ref, fresh
):
    steps = step_ref.shape[2]
    shard, column = lax.div(tile, 4), lax.rem(tile, 4)
    cols = pl.ds(pl.multiple_of(tile * LANES, LANES), LANES)
    lanes = pl.ds(pl.multiple_of(column * LANES, LANES), LANES)
    first = ROW_RATE + 16 * branch
    skip = jnp.broadcast_to(
        rest_ref[shard, ROW_SKIP + branch : ROW_SKIP + branch + 1, lanes], (CHUNKS, LANES)
    )
    for start in (0, 8):
        rates = jnp.stack(
            [
                jnp.broadcast_to(
                    rest_ref[shard, first + n : first + n + 1, lanes], (CHUNKS, LANES)
                )
                for n in range(start, start + 8)
            ]
        )
        state = jnp.zeros((8, CHUNKS, LANES), F32)
        elapsed = jnp.zeros((CHUNKS, LANES), F32)
        for j in range(steps):
            t = j if branch == 0 else steps - 1 - j
            size = step_ref[branch, tile, t]
            u = u_ref[branch, pl.ds(t * CHUNKS, CHUNKS), cols].astype(F32)
            at = pl.ds((t * 16 + start) * CHUNKS, 8 * CHUNKS)
            into = in_wide[branch, at, :].reshape(8, CHUNKS, LANES)
            out = out_wide[branch, at, :].reshape(8, CHUNKS, LANES)
            state = jnp.exp2(rates * size[None]) * state + (size * u)[None] * into
            part = jnp.sum(out * state, axis=0)
            if start == 0:
                part = part + skip * u
                elapsed = elapsed + size
            if start > 0 or not fresh:
                part = part + y_ref[tile, t]
            y_ref[tile, t] = part
        if start == 0 and fresh:
            total_ref[branch, tile] = elapsed
        end_ref[branch, tile, start * CHUNKS : (start + 8) * CHUNKS, :] = state.reshape(
            8 * CHUNKS, LANES
        )


def chunk_states(branch, tile, u_ref, rest_ref, step_ref, in_half, end_ref, total_ref):
    steps = step_ref.shape[2]
    shard, column = lax.div(tile, 4), lax.rem(tile, 4)
    cols = pl.ds(pl.multiple_of(tile * LANES, LANES), LANES)
    lanes = pl.ds(pl.multiple_of(column * LANES, LANES), LANES)
    first = ROW_RATE + 16 * branch
    rates = [
        jnp.broadcast_to(rest_ref[shard, first + n : first + n + 1, lanes], (16, LANES)).astype(BF16)
        for n in range(16)
    ]
    states = [None] * 16
    left = jnp.zeros((CHUNKS, LANES), F32)
    for j in range(0, steps, 2):
        pair, sizes = [], []
        for i in (j, j + 1):
            t = steps - 1 - i if branch == 0 else i
            size = step_ref[branch, tile, t]
            pair.append(left)
            sizes.append(size)
            left = left + size
        low = steps - 2 - j if branch == 0 else j
        if branch == 0:
            pair, sizes = pair[::-1], sizes[::-1]
        spans = jnp.concatenate(pair, 0).astype(BF16)
        drive = jnp.concatenate(sizes, 0).astype(BF16) * u_ref[branch, low * CHUNKS : (low + 2) * CHUNKS, cols]
        for n in range(16):
            at = ((low // 2) * 16 + n) * 16
            part = jnp.exp2(rates[n] * spans) * (drive * in_half[branch, at : at + 16, :])
            states[n] = part if states[n] is None else states[n] + part
    total_ref[branch, tile] = left
    for n in range(16):
        state = states[n].astype(F32)
        end_ref[branch, tile, n * CHUNKS : (n + 1) * CHUNKS, :] = state[:CHUNKS] + state[CHUNKS:]


def device_state(branch, tile, rest_ref, end_ref, total_ref):
    shard, column = lax.div(tile, 4), lax.rem(tile, 4)
    lanes = pl.ds(pl.multiple_of(column * LANES, LANES), LANES)
    first = ROW_RATE + 16 * branch
    rates = rest_ref[shard, first : first + 16, lanes]
    state = jnp.zeros((16, LANES), F32)
    elapsed = jnp.zeros((1, LANES), F32)
    for j in range(CHUNKS):
        k = j if branch == 0 else CHUNKS - 1 - j
        span = total_ref[branch, tile, k : k + 1, :]
        state = jnp.exp2(rates * span) * state + end_ref[branch, tile, pl.ds(k, 16, stride=CHUNKS), :]
        elapsed = elapsed + span
    return state, elapsed


def as_message(state, elapsed):
    high = elapsed.astype(BF16).astype(F32)
    low = elapsed - high
    row = iota((16, LANES), 0)
    times = jnp.where(row == 0, high, jnp.where(row == 1, low, 0.0))
    return jnp.concatenate([state, times], 0).astype(BF16)


def of_message(message):
    values = message.astype(F32)
    return values[0:16], values[16:17] + values[17:18]


def chunk_carries(branch, tile, rest_ref, end_ref, carry, total_ref):
    shard, column = lax.div(tile, 4), lax.rem(tile, 4)
    lanes = pl.ds(pl.multiple_of(column * LANES, LANES), LANES)
    first = ROW_RATE + 16 * branch
    rates = rest_ref[shard, first : first + 16, lanes]
    carries = []
    for j in range(CHUNKS):
        k = j if branch == 0 else CHUNKS - 1 - j
        carries.append((k, carry))
        if j < CHUNKS - 1:
            carry = (
                jnp.exp2(rates * total_ref[branch, tile, k : k + 1, :]) * carry
                + end_ref[branch, tile, pl.ds(k, 16, stride=CHUNKS), :]
            )
    return carries


def correct_tile(branch, tile, rest_ref, step_ref, out_half, y_ref, chunk_carry):
    shard, column = lax.div(tile, 4), lax.rem(tile, 4)
    lanes = pl.ds(pl.multiple_of(column * LANES, LANES), LANES)
    first = ROW_RATE + 16 * branch
    steps = step_ref.shape[2]
    entering = []
    wide = []
    for n in range(16):
        one = chunk_carry[n * CHUNKS : (n + 1) * CHUNKS, :]
        entering.append(jnp.concatenate([one, one], 0).astype(BF16))
        rate = rest_ref[shard, first + n : first + n + 1, lanes]
        wide.append(jnp.broadcast_to(rate, (16, LANES)).astype(BF16))
    elapsed = jnp.zeros((CHUNKS, LANES), F32)
    for j in range(0, steps, 2):
        pair = []
        for i in (j, j + 1):
            t = i if branch == 0 else steps - 1 - i
            elapsed = elapsed + step_ref[branch, tile, t]
            pair.append(elapsed)
        low = j if branch == 0 else steps - 2 - j
        if branch == 1:
            pair = pair[::-1]
        spans = jnp.concatenate(pair, 0).astype(BF16)
        total = None
        for n in range(16):
            at = ((low // 2) * 16 + n) * 16
            part = jnp.exp2(wide[n] * spans) * entering[n] * out_half[branch, at : at + 16, :]
            total = part if total is None else total + part
        total = total.astype(F32)
        y_ref[tile, low] = y_ref[tile, low] + total[:CHUNKS]
        y_ref[tile, low + 1] = y_ref[tile, low + 1] + total[CHUNKS:]


def mix_tile(tile, y_ref, result_ref, rows_f32):
    steps = y_ref.shape[1]
    rows = result_ref.shape[0]
    cols = pl.ds(pl.multiple_of(tile * LANES, LANES), LANES)
    for t in range(steps):
        rows_f32[pl.ds(t, CHUNKS, stride=steps), :] = y_ref[tile, t]
    result_ref[:, cols] = rows_f32[0:rows, :].astype(BF16)


def whole_kernel(
    x_hbm, conv_own, bias_own, proj_own, step_own, shift_own, rate_own, skip_own, result_ref,
    rows_ref, conv_in, bias_in, shift_in, rate_in, skip_in,
    conv_ref, proj_weight_ref, rest_ref, step_weight_ref,
    u_ref, rows_f32, in_wide, out_wide, in_half, out_half, step_ref, y_ref, end_ref, total_ref, chunk_carry,
    mine_state, mine_time, out0, in0, out1, in1, out2, in2, out3, in3, out4, in4, own_carry,
    local_state, local_time,
    local_sem, halo_send, halo_recv, gather_send, gather_recv,
    send0, recv0, send1, recv1, send2, recv2, send3, recv3, send4, recv4, known,
):
    s, g = lax.axis_index("seq"), lax.axis_index("grp")
    seq, grp = lax.axis_size("seq"), lax.axis_size("grp")
    y, core = lax.div(g, 2), lax.rem(g, 2)
    other = 1 - core
    y_left, y_right, y_far = lax.rem(y + 3, 4), lax.rem(y + 1, 4), lax.rem(y + 2, 4)
    group, x = lax.div(s, 4), lax.rem(s, 4)
    chip = x * 4 + y
    chips, groups = 16, seq // 4
    flip = 4 - 8 * lax.rem(group, 2)
    right = (s + lax.div(y + 1, 4) * flip, y_right * 2 + core)
    left = (s + (1 - lax.div(y + 3, 4)) * flip, y_left * 2 + core)
    sibling = (s, y * 2 + other)
    right_far = (s + lax.div(y + 2, 4) * flip, y_far * 2 + core)
    left_far = (s + (1 - lax.div(y + 2, 4)) * flip, y_far * 2 + core)
    place = s * grp + g
    count = seq * grp
    after, before = lax.rem(place + 1, count), lax.rem(place + count - 1, count)
    after, before = (lax.div(after, grp), lax.rem(after, grp)), (lax.div(before, grp), lax.rem(before, grp))

    def chip_at(k):
        return (group * 4 + lax.div(k, 4), lax.rem(k, 4) * 2 + core)

    def group_at(k):
        return (k * 4 + x, g)

    def remote(src, dst, send, recv, device):
        return pltpu.make_async_remote_copy(
            src_ref=src, dst_ref=dst, send_sem=send, recv_sem=recv, device_id=device,
            device_id_type=MESH,
        )

    rows = x_hbm.shape[0]
    small_copies = [
        pltpu.make_async_copy(src, dst, local_sem.at[k])
        for k, (src, dst) in enumerate(
            [(conv_own, conv_in), (bias_own, bias_in), (shift_own, shift_in), (rate_own, rate_in),
             (skip_own, skip_in)]
        )
    ]
    rows_copy = pltpu.make_async_copy(x_hbm, rows_ref.at[HALO : HALO + rows], local_sem.at[5])
    proj_copy = pltpu.make_async_copy(proj_own, proj_weight_ref.at[g], local_sem.at[6])
    step_copy = pltpu.make_async_copy(step_own, step_weight_ref.at[g], local_sem.at[7])
    for copy in small_copies:
        copy.start()
    rows_copy.start()
    proj_copy.start()
    step_copy.start()

    barrier = pltpu.get_barrier_semaphore()

    def greet(device):
        pl.semaphore_signal(barrier, inc=1, device_id=device, device_id_type=MESH)

    for device in (right, left, right_far, left_far, after, before, sibling):
        greet(device)
    for d in range(1, chips):
        greet(chip_at(lax.rem(chip + d, chips)))
    high = lax.rem(group, 2)
    next_group = group_at(lax.rem(group + 2, groups))
    last_group = group_at(lax.rem(group + groups - 2, groups))
    high_group = group_at(group + 1 - 2 * high)
    for device in (next_group, last_group, high_group):
        greet(device)

    for copy in small_copies:
        copy.wait()
    width = conv_in.shape[-1]
    conv_ref[g, 0:4, :] = conv_in[0]
    conv_ref[g, 4:8, :] = conv_in[1]
    conv_ref[g, 8:10, :] = bias_in[...]
    conv_ref[g, 10:16, :] = jnp.zeros((6, width), F32)
    rest_ref[g, 0:2, :] = shift_in[...]
    rest_ref[g, 2:4, :] = skip_in[...]
    rest_ref[g, 4:8, :] = jnp.zeros((4, width), F32)
    rest_ref[g, 8:24, :] = rate_in[0] * -LOG2E
    rest_ref[g, 24:40, :] = rate_in[1] * -LOG2E
    pl.semaphore_wait(barrier, 10 + chips - 1)

    def pass_on(turn):
        for device in (next_group, last_group) if turn < 3 else (high_group,):
            pl.semaphore_signal(known.at[turn], inc=1, device_id=device, device_id_type=MESH)

    def learn(turn):
        pl.semaphore_wait(known.at[turn], 2 if turn < 3 else 1)

    pass_on(0)

    halos = [
        remote(x_hbm.at[rows - HALO : rows], rows_ref.at[0:HALO], halo_send.at[0], halo_recv.at[0], after),
        remote(
            x_hbm.at[0:HALO], rows_ref.at[HALO + rows : 2 * HALO + rows], halo_send.at[1],
            halo_recv.at[1], before,
        ),
    ]
    whole = (conv_ref, proj_weight_ref, rest_ref, step_weight_ref, proj_weight_ref, step_weight_ref)
    own = (
        conv_ref.at[g], proj_own.at[0], rest_ref.at[g], step_own.at[0], proj_own.at[1], step_own.at[1]
    )
    branch_of = (None, 0, None, 0, 1, 1)
    cuts = ((0, 8, 16), (0, 80, 160), (0, 24, 40), (0, 64, 128), (0, 80, 160), (0, 64, 128))

    def part(kind, slot, half):
        low, high = (0, cuts[kind][2]) if half is None else cuts[kind][half : half + 2]
        if branch_of[kind] is None:
            return whole[kind].at[slot, low:high]
        return whole[kind].at[slot, branch_of[kind], low:high]

    sent_slot = (g, g, y_left * 2 + core, y_right * 2 + core, g, y_left * 2 + core,
                 y_right * 2 + core, y_far * 2 + core, y_far * 2 + core)
    got_slot = (y_left * 2 + core, y_right * 2 + core, y_far * 2 + core, y_far * 2 + core,
                y * 2 + other, y_left * 2 + other, y_right * 2 + other, y_far * 2 + other,
                y_far * 2 + other)
    halves = (None, None, 0, 1, None, None, None, 0, 1)
    targets = (right, left, right, left) + (sibling,) * 5

    def outgoing(kind, way):
        target = targets[way]
        if kind in DIRECT and way in (2, 3):
            dst = part(kind, g, halves[way])
            src = own_part(kind, halves[way])
            target = right_far if way == 2 else left_far
        else:
            dst = part(kind, sent_slot[way], halves[way])
            src = own[kind] if way in (0, 1, 4) else dst
        return remote(src, dst, gather_send.at[kind, way], gather_recv.at[kind, way], target)

    def arrived(kind, way):
        dst = part(kind, got_slot[way], halves[way])
        remote(dst, dst, gather_send.at[kind, way], gather_recv.at[kind, way], targets[way]).wait_recv()

    def own_part(kind, half):
        return own[kind].at[cuts[kind][half] : cuts[kind][half + 1]]

    def send_own(kind):
        for way in (0, 1, 2, 3, 4) if kind in DIRECT else (0, 1, 4):
            outgoing(kind, way).start()

    def forward_near(kind):
        for way in (0, 1):
            arrived(kind, way)
            if kind not in DIRECT:
                outgoing(kind, 2 + way).start()
            outgoing(kind, 5 + way).start()

    def forward_far(kind):
        arrived(kind, 2)
        outgoing(kind, 7).start()
        arrived(kind, 3)
        outgoing(kind, 8).start()

    send_own(0)
    for copy in halos:
        copy.start()
    send_own(1)

    first = jnp.where(place == 0, 0.0, 1.0).astype(F32)
    last = jnp.where(place == count - 1, 0.0, 1.0).astype(F32)
    tiles_chip = 8

    def conv_chip(at):
        def body(i, _):
            convolve(at * tiles_chip + i, rows_ref, first, last, conv_ref, u_ref, rows_f32.at[0])
            return 0

        lax.fori_loop(0, tiles_chip, body, 0)

    forward_near(0)
    rows_copy.wait()
    for copy in halos:
        copy.wait_recv()
    arrived(0, 4)
    conv_chip(y)
    learn(0)
    pass_on(1)
    arrived(0, 5)
    conv_chip(y_left)
    forward_far(0)
    arrived(0, 6)
    conv_chip(y_right)
    learn(1)
    pass_on(2)
    arrived(0, 7)
    arrived(0, 8)
    conv_chip(y_far)

    lows = [None, None]

    def project(branch, at, total):
        for i in range(2):
            shard = at * 2 + i
            cols = pl.ds(pl.multiple_of(shard * width, width), width)
            total = total + dot_t(u_ref[branch, :, cols], proj_weight_ref[shard, branch])
        return total

    def project_all(branch, kind):
        arrived(kind, 4)
        total = project(branch, y, jnp.zeros((rows, proj_weight_ref.shape[2]), F32))
        arrived(kind, 5)
        total = project(branch, y_left, total)
        if kind == 1:
            forward_far(kind)
        arrived(kind, 6)
        total = project(branch, y_right, total)
        arrived(kind, 7)
        arrived(kind, 8)
        projected = project(branch, y_far, total).astype(BF16)
        spread_maps(branch, projected[:, 128:160], in_wide, out_wide, in_half, out_half)
        lows[branch] = projected[:, 0:128]

    def steps_of(branch, at):
        for i in range(2):
            step_sizes(branch, at * 2 + i, lows[branch], step_weight_ref, rest_ref, step_ref)

    def scan(branch, at, start=0, stop=tiles_chip):
        def body(i, _):
            scan_tile(
                branch, at * tiles_chip + i, u_ref, rest_ref, step_ref, in_wide, out_wide, y_ref,
                end_ref, total_ref, branch == 0,
            )
            return 0

        lax.fori_loop(start, stop, body, 0)

    def states_of(branch, at):
        def body(i, _):
            chunk_states(
                branch, at * tiles_chip + i, u_ref, rest_ref, step_ref, in_half, end_ref, total_ref
            )
            return 0

        lax.fori_loop(0, tiles_chip, body, 0)

    def to_core(branch, at):
        span = pl.ds(at * 4, 4)
        return remote(
            out0.at[branch, span], in0.at[branch, span], send0.at[branch, at], recv0.at[branch, at],
            sibling,
        )

    def finish(branch, at):
        span = range(4)
        mine = [
            device_state(branch, 2 * (at * 4 + i) + core, rest_ref, end_ref, total_ref) for i in span
        ]
        theirs = [
            as_message(*device_state(branch, 2 * (at * 4 + i) + other, rest_ref, end_ref, total_ref))
            for i in span
        ]
        for i in span:
            out0[branch, at * 4 + i] = theirs[i]
        to_core(branch, at).start()
        for i in span:
            mine_state[branch, at * 4 + i] = mine[i][0]
            mine_time[branch, at * 4 + i] = jnp.broadcast_to(mine[i][1], (8, LANES))

    def rates_of(branch, k):
        tile = 2 * k + core
        low = ROW_RATE + 16 * branch
        lanes = pl.ds(pl.multiple_of(lax.rem(tile, 4) * LANES, LANES), LANES)
        return rest_ref[lax.div(tile, 4), low : low + 16, lanes]

    def in_order(branch, k):
        here = (mine_state[branch, k], mine_time[branch, k, 0:1, :])
        there = of_message(in0[branch, k])
        leads = core == branch
        return [
            jnp.where(leads, a, b)
            for a, b in ((here[0], there[0]), (here[1], there[1]), (there[0], here[0]), (there[1], here[1]))
        ]

    def to_chip(branch, k):
        return remote(
            out1.at[branch, k], in1.at[branch, chip], send1.at[branch, k], recv1.at[branch, chip],
            chip_at(k),
        )

    def relay(branch, at):
        to_core(branch, at).wait_recv()
        messages = []
        for i in range(4):
            k = at * 4 + i
            state1, time1, state2, time2 = in_order(branch, k)
            state = jnp.exp2(rates_of(branch, k) * time2) * state1 + state2
            messages.append(as_message(state, time1 + time2))
        for i in range(4):
            out1[branch, at * 4 + i] = messages[i]
        for i in range(4):
            k = at * 4 + i

            @pl.when(k != chip)
            def _():
                to_chip(branch, k).start()

    def combine_chips(branch):
        for d in range(1, chips):
            k = lax.rem(chip + chips - d, chips)
            remote(
                in1.at[branch, k], in1.at[branch, k], send1.at[branch, k], recv1.at[branch, k], chip_at(k)
            ).wait_recv()
        in1[branch, chip] = out1[branch, chip]
        rates = rates_of(branch, chip)
        state = jnp.zeros((16, LANES), F32)
        elapsed = jnp.zeros((1, LANES), F32)
        entering = []
        for j in range(chips):
            k = j if branch == 0 else chips - 1 - j
            entering.append((k, state, elapsed))
            gained, span = of_message(in1[branch, k])
            state = jnp.exp2(rates * span) * state + gained
            elapsed = elapsed + span
        out2[branch] = as_message(state, elapsed)
        for d in range(1, groups):
            k = lax.rem(group + d, groups)
            remote(
                out2.at[branch], in2.at[branch, group], send2.at[branch, k], recv2.at[branch, group],
                group_at(k),
            ).start()
        for k, state, elapsed in entering:
            local_state[branch, k] = state
            local_time[branch, k] = jnp.broadcast_to(elapsed, (8, LANES))

    def combine_groups(branch):
        for d in range(1, groups):
            k = lax.rem(group + groups - d, groups)
            remote(
                in2.at[branch, k], in2.at[branch, k], send2.at[branch, k], recv2.at[branch, k], group_at(k)
            ).wait_recv()
        in2[branch, group] = out2[branch]
        rates = rates_of(branch, chip)
        state = jnp.zeros((16, LANES), F32)
        for j in range(groups):
            k = j if branch == 0 else groups - 1 - j
            gained, span = of_message(in2[branch, k])
            new = jnp.exp2(rates * span) * state + gained
            state = jnp.where(k < group if branch == 0 else k > group, new, state)
        for k in range(chips):
            out3[branch, k] = (
                jnp.exp2(rates * local_time[branch, k, 0:1, :]) * state + local_state[branch, k]
            ).astype(BF16)
        for d in range(1, chips):
            k = lax.rem(chip + d, chips)
            remote(
                out3.at[branch, k], in3.at[branch, chip], send3.at[branch, k], recv3.at[branch, chip],
                chip_at(k),
            ).start()

    def back_to_core(branch):
        return remote(out4.at[branch], in4.at[branch], send4.at[branch], recv4.at[branch], sibling)

    def receive(branch):
        for d in range(1, chips):
            k = lax.rem(chip + chips - d, chips)
            remote(
                in3.at[branch, k], in3.at[branch, k], send3.at[branch, k], recv3.at[branch, k], chip_at(k)
            ).wait_recv()
        in3[branch, chip] = out3[branch, chip]
        leads = core == branch
        for low in range(0, chips, 4):
            pairs = []
            for k in range(low, low + 4):
                carry = in3[branch, k].astype(F32)
                state1, time1, _, _ = in_order(branch, k)
                second = jnp.exp2(rates_of(branch, k) * time1) * carry + state1
                pairs.append((jnp.where(leads, carry, second), jnp.where(leads, second, carry)))
            for k in range(low, low + 4):
                own_carry[branch, k] = pairs[k - low][0].astype(BF16)
                out4[branch, k] = pairs[k - low][1].astype(BF16)
        back_to_core(branch).start()

    def correct(branch, mine, start, stop):
        held = own_carry if mine else in4

        def body(i, _):
            places = [(q, 2 * (2 * i + q) + (core if mine else other)) for q in range(2)]
            carries = [
                chunk_carries(
                    branch, tile, rest_ref, end_ref, held[branch, 2 * i + q].astype(F32), total_ref
                )
                for q, tile in places
            ]
            for q, tile in places:
                for k, carry in carries[q]:
                    chunk_carry[q, pl.ds(k, 16, stride=CHUNKS), :] = carry
            for q, tile in places:
                correct_tile(branch, tile, rest_ref, step_ref, out_half, y_ref, chunk_carry.at[q])
                if branch == 1:
                    mix_tile(tile, y_ref, result_ref, rows_f32.at[q])
            return 0

        lax.fori_loop(start // 2, stop // 2, body, 0)

    forward_near(1)
    send_own(2)
    send_own(3)
    proj_copy.wait()
    project_all(0, 1)
    learn(2)
    pass_on(3)

    step_copy.wait()
    arrived(2, 4)
    arrived(3, 4)
    steps_of(0, y)
    forward_near(2)
    forward_near(3)
    send_own(4)
    send_own(5)
    scan(0, y)
    learn(3)
    finish(0, y)
    arrived(2, 5)
    arrived(3, 5)
    steps_of(0, y_left)
    forward_far(2)
    forward_far(3)
    relay(0, y)
    scan(0, y_left)
    finish(0, y_left)
    arrived(2, 6)
    arrived(3, 6)
    steps_of(0, y_right)
    relay(0, y_left)
    scan(0, y_right, 0, 4)
    forward_near(4)
    scan(0, y_right, 4, 8)
    finish(0, y_right)
    for kind in (2, 3):
        for way in (7, 8):
            arrived(kind, way)
    steps_of(0, y_far)
    relay(0, y_right)
    scan(0, y_far, 0, 4)
    forward_near(5)
    forward_far(4)
    scan(0, y_far, 4, 8)
    finish(0, y_far)
    project_all(1, 4)
    relay(0, y_far)
    arrived(5, 4)
    steps_of(1, y)
    forward_far(5)
    states_of(1, y)
    finish(1, y)
    arrived(5, 5)
    steps_of(1, y_left)
    relay(1, y)
    states_of(1, y_left)
    finish(1, y_left)
    arrived(5, 6)
    steps_of(1, y_right)
    relay(1, y_left)
    states_of(1, y_right)
    finish(1, y_right)
    combine_chips(0)
    arrived(5, 7)
    arrived(5, 8)
    steps_of(1, y_far)
    relay(1, y_right)
    states_of(1, y_far)
    finish(1, y_far)
    scan(1, y, 0, 4)
    relay(1, y_far)
    scan(1, y, 4, 8)
    scan(1, y_left)
    combine_groups(0)
    scan(1, y_right, 0, 4)
    combine_chips(1)
    scan(1, y_right, 4, 8)
    scan(1, y_far)
    receive(0)
    correct(0, True, 0, 16)
    combine_groups(1)
    back_to_core(0).wait_recv()
    correct(0, False, 0, 16)
    receive(1)
    correct(1, True, 0, 16)
    back_to_core(1).wait_recv()
    correct(1, False, 0, 16)

    for copy in halos:
        copy.wait_send()
    for kind in range(6):
        for way in range(9):
            outgoing(kind, way).wait_send()
    for branch in range(2):
        for at in range(4):
            to_core(branch, at).wait_send()
        back_to_core(branch).wait_send()
        for d in range(1, chips):
            k = lax.rem(chip + d, chips)
            for source, send in ((out1, send1), (out3, send3)):
                remote(
                    source.at[branch, k], source.at[branch, k], send.at[branch, k], recv1.at[branch, k],
                    chip_at(k),
                ).wait_send()
        for d in range(1, groups):
            k = lax.rem(group + d, groups)
            remote(
                out2.at[branch], out2.at[branch], send2.at[branch, k], recv2.at[branch, k], group_at(k)
            ).wait_send()


def run_whole(x, conv_weight, conv_bias, proj_weight, step_weight, step_bias, decay_rate, skip_gain):
    rows, channels = x.shape
    width = conv_weight.shape[2]
    tiles, steps = channels // LANES, rows // CHUNKS
    shards = lax.axis_size("grp")
    chips = 2 * shards
    groups = lax.axis_size("seq") // 4
    anywhere = pl.BlockSpec(memory_space=pl.ANY)
    vmem, dma = pltpu.VMEM, pltpu.SemaphoreType.DMA
    return pl.pallas_call(
        whole_kernel,
        out_shape=jax.ShapeDtypeStruct((rows, channels), BF16),
        in_specs=[anywhere] * 8,
        out_specs=pl.BlockSpec(memory_space=pltpu.VMEM),
        scratch_shapes=[
            vmem((rows + 2 * HALO, channels), BF16),
            vmem(conv_weight.shape, F32),
            vmem(conv_bias.shape, F32),
            vmem(step_bias.shape, F32),
            vmem(decay_rate.shape, F32),
            vmem(skip_gain.shape, F32),
            vmem((shards, ROWS_CONV, width), F32),
            vmem((shards,) + proj_weight.shape, BF16),
            vmem((shards, ROWS_REST, width), F32),
            vmem((shards,) + step_weight.shape, BF16),
            vmem((2, rows, channels), BF16),
            vmem((2, rows + 2 * HALO, LANES), F32),
            vmem((2, rows * 16, LANES), F32),
            vmem((2, rows * 16, LANES), F32),
            vmem((2, rows * 16, LANES), BF16),
            vmem((2, rows * 16, LANES), BF16),
            vmem((2, tiles, steps, CHUNKS, LANES), F32),
            vmem((tiles, steps, CHUNKS, LANES), F32),
            vmem((2, tiles, 16 * CHUNKS, LANES), F32),
            vmem((2, tiles, CHUNKS, LANES), F32),
            vmem((2, 16 * CHUNKS, LANES), F32),
            vmem((2, chips, 16, LANES), F32),
            vmem((2, chips, 8, LANES), F32),
            vmem((2, chips, 32, LANES), BF16),
            vmem((2, chips, 32, LANES), BF16),
            vmem((2, chips, 32, LANES), BF16),
            vmem((2, chips, 32, LANES), BF16),
            vmem((2, 32, LANES), BF16),
            vmem((2, groups, 32, LANES), BF16),
            vmem((2, chips, 16, LANES), BF16),
            vmem((2, chips, 16, LANES), BF16),
            vmem((2, chips, 16, LANES), BF16),
            vmem((2, chips, 16, LANES), BF16),
            vmem((2, chips, 16, LANES), BF16),
            vmem((2, chips, 16, LANES), F32),
            vmem((2, chips, 8, LANES), F32),
            dma((8,)),
            dma((2,)),
            dma((2,)),
            dma((6, 9)),
            dma((6, 9)),
            dma((2, 4)),
            dma((2, 4)),
            dma((2, chips)),
            dma((2, chips)),
            dma((2, groups)),
            dma((2, groups)),
            dma((2, chips)),
            dma((2, chips)),
            dma((2,)),
            dma((2,)),
            pltpu.SemaphoreType.REGULAR((4,)),
        ],
        compiler_params=pltpu.CompilerParams(
            vmem_limit_bytes=56 << 20, collective_id=0, has_side_effects=True
        ),
    )(x, conv_weight, conv_bias, proj_weight, step_weight, step_bias, decay_rate, skip_gain)


def local(
    inner_input,
    inner_gate,
    conv_weight,
    conv_bias,
    proj_weight,
    step_weight,
    step_bias,
    decay_rate,
    skip_gain,
):
    mixed = run_whole(
        inner_input, conv_weight, conv_bias, jnp.swapaxes(proj_weight, 1, 2), step_weight, step_bias,
        decay_rate, skip_gain,
    )
    return (mixed.astype(F32) * jax.nn.silu(inner_gate.astype(F32))).astype(BF16)


def solution(mesh):
    placed = (
        P(("seq", "grp"), None),
        P(("seq", "grp"), None),
        P(None, None, "grp"),
        P(None, "grp"),
        P(None, "grp", None),
        P(None, None, "grp"),
        P(None, "grp"),
        P(None, None, "grp"),
        P(None, "grp"),
    )
    return jax.shard_map(
        local, mesh=mesh, in_specs=placed, out_specs=P(("seq", "grp"), None), check_vma=False
    )
```
